512 devices in a mesh: rec: 16 (over z, core), frame: 32 (over x, y).
Axes of the slice: x: 4, y: 8, z: 8, core: 2. Of those that a mesh axis runs over, the one named last changes fastest.
Arguments:
- frames: bfloat16 [16, 49152, 256], P('rec', 'frame'), may hold values from -10 to 10
- texts: bfloat16 [32, 224, 256], P('rec', 'frame'), may hold values from -100 to 100
- pair_rec: int32 [32, 1], replicated, may hold values from 0 to 15, as said below
- pair_text: int32 [32], replicated, may hold values from 0 to 31, as said below
- pair_label: int32 [32], replicated, may hold values 0 or 1
Outputs:
- loss: float32 [], replicated
- grad_frames: bfloat16 [16, 49152, 256], P('rec', 'frame')
- grad_texts: bfloat16 [32, 224, 256], P('rec', 'frame')
The draws below stay inside these ranges and needn't reach their ends.
Inputs may be any that keep to these rules, and one draw needn't show every extreme that they name: `pair_rec`: no recording is named by more than 6 pairs, some recording by exactly 6, and every recording by at least one. A pair's text is held by the index of rec one after, one before, or 8 after its recording (counted round): pair_text // 2 = (pair_rec + k) mod 16 with k one of 1, 15, 8.
All inputs are finite; a program needn't handle non-finite values.
Results may differ from the reference program's by a relative error of at most 0.0085.
Values may be sent and summed in bfloat16 or wider, within the bound.
A program may use at most 64 MiB of HBM per device.

```python
import jax
import jax.numpy as jnp
from jax import lax

D = 256
L = 224
MOST = 6
TXT_DEV = 2
RECS = 16
FRAMES = 49152
TEXTS = 32
PAIRS = 32


LOG_EIGHT = 2.0794415


def recording_offset(key):
    direction = jnp.clip(jax.random.normal(jax.random.fold_in(key, 5), (RECS, D), jnp.float32), -4.0, 4.0)
    strength = jax.random.uniform(jax.random.fold_in(key, 6), (RECS, 1), jnp.float32, 0.3, 0.9)
    return strength * direction


def token_scales(key, top):
    exponent = jax.random.uniform(jax.random.fold_in(key, 7), (TEXTS, L, 1), jnp.float32, 0.0, top)
    return jnp.exp(exponent)


def draw_frames(key, part):
    offset = recording_offset(key)
    base = jnp.clip(jax.random.normal(jax.random.fold_in(key, 1), (RECS, FRAMES, D), jnp.float32), -6.0, 6.0)
    base = base + offset[:, None, :]
    return jnp.clip(base, -10.0, 10.0).astype(jnp.bfloat16)


def draw_texts(key, part):
    base = jnp.clip(jax.random.normal(jax.random.fold_in(key, 3), (TEXTS, L, D), jnp.float32), -6.0, 6.0)
    base = base * token_scales(key, LOG_EIGHT)
    return base.astype(jnp.bfloat16)


def pair_lists(key):
    order_table = jax.random.permutation(jax.random.fold_in(key, 211), RECS).astype(jnp.int32)
    position = jnp.arange(RECS, dtype=jnp.int32)
    extra_count = PAIRS - MOST - (RECS - 1)
    counts = jnp.where(position == 0, MOST, 1 + ((position >= 1) & (position <= extra_count)).astype(jnp.int32))
    boundary = jnp.cumsum(counts)
    pair_index = jnp.arange(PAIRS, dtype=jnp.int32)
    group_index = jnp.sum((pair_index[:, None] >= boundary[None, :]).astype(jnp.int32), axis=1)
    record = order_table[group_index]
    shuffle = jax.random.permutation(jax.random.fold_in(key, 223), PAIRS)
    record = record[shuffle]
    offset_draw = jax.random.randint(jax.random.fold_in(key, 227), (PAIRS,), 0, 8)
    offset = jnp.where(offset_draw < 3, 1, jnp.where(offset_draw < 6, RECS - 1, RECS // 2))
    text_owner = (record + offset) % RECS
    pair_texts = TXT_DEV * text_owner + jax.random.randint(jax.random.fold_in(key, 229), (PAIRS,), 0, TXT_DEV)
    return (record.astype(jnp.int32), pair_texts.astype(jnp.int32))


def draw_pair_rec(key, part):
    record, pair_texts = pair_lists(key)
    return record[:, None]


def draw_pair_text(key, part):
    record, pair_texts = pair_lists(key)
    return pair_texts


def touch_ends(result, rng, low, top_value):
    index_at = [jax.random.randint(jax.random.fold_in(rng, axis), (), 0, length) for axis, length in enumerate(result.shape)]
    main_axis = result.shape.index(max(result.shape))
    beside = index_at[:main_axis] + [(index_at[main_axis] + 1) % result.shape[main_axis]] + index_at[main_axis + 1:]
    return result.at[tuple(index_at)].set(low).at[tuple(beside)].set(top_value)


def setup_inputs(seed: int = 0) -> dict:
    seeds = jax.random.split(jax.random.key(seed), 6)
    return {
        "frames": draw_frames(jax.random.fold_in(seeds[5], 71), 0),
        "texts": draw_texts(jax.random.fold_in(seeds[5], 71), 0),
        "pair_rec": draw_pair_rec(jax.random.fold_in(seeds[5], 71), 0),
        "pair_text": draw_pair_text(jax.random.fold_in(seeds[5], 71), 0),
        "pair_label": touch_ends((jax.random.randint(seeds[4], (PAIRS,), 0, 2) < 1).astype(jnp.int32), jax.random.fold_in(seeds[4], 1), 0, 1),
    }


EPS = 1e-06
TEMP = 10.0
BIAS = -1.0
LOSS_SCALE = 2048.0

def slot_tables(pair_rec, pair_text, pair_label, here, most):
    record = pair_rec[:, 0]
    count = record.shape[0]
    order = jnp.arange(count, dtype=jnp.int32)
    same = (record[:, None] == record[None, :]).astype(jnp.int32)
    earlier = (order[None, :] < order[:, None]).astype(jnp.int32)
    rank = lax.optimization_barrier(jnp.sum(same * earlier, axis=1))
    places = jnp.arange(most, dtype=jnp.int32)
    chosen = ((record[None, :] == here) & (rank[None, :] == places[:, None])).astype(jnp.int32)
    valid = lax.optimization_barrier(jnp.sum(chosen, axis=1))
    slot_text = lax.optimization_barrier(jnp.sum(chosen * pair_text[None, :], axis=1))
    sign = lax.optimization_barrier(jnp.sum(chosen * (2 * pair_label[None, :] - 1), axis=1))
    return (valid, slot_text, sign)

def slot_pass(upstream_signal, query_vectors, valid, sign):
    logit_scale = D ** (-0.5)
    pair_scores = jnp.dot(query_vectors, upstream_signal.T, preferred_element_type=jnp.float32) * logit_scale
    row_max = lax.optimization_barrier(jnp.max(pair_scores, axis=1))
    expo = jnp.exp(pair_scores - row_max[:, None])
    batch_weights = expo.astype(jnp.bfloat16)
    context = jnp.dot(batch_weights, upstream_signal, preferred_element_type=jnp.float32)
    query_f = query_vectors.astype(jnp.float32)
    q_norm = lax.rsqrt(lax.optimization_barrier(jnp.sum(query_f * query_f, axis=1)) + EPS)
    c_norm = lax.rsqrt(lax.optimization_barrier(jnp.sum(context * context, axis=1)) + EPS)
    q_unit = query_f * q_norm[:, None]
    c_unit = context * c_norm[:, None]
    cos = lax.optimization_barrier(jnp.sum(q_unit * c_unit, axis=1))
    score = jnp.mean(cos)
    margin = -sign * (TEMP * score + BIAS)
    loss_part = valid * jax.nn.softplus(margin)
    grad_cos = -LOSS_SCALE * TEMP * valid * sign * jax.nn.sigmoid(margin) / L
    d_context = grad_cos * (q_unit - cos[:, None] * c_unit) * c_norm[:, None]
    direct = grad_cos * (c_unit - cos[:, None] * q_unit) * q_norm[:, None]
    context_batch_gradient = d_context.astype(jnp.bfloat16)
    weight_gradient = jnp.dot(context_batch_gradient, upstream_signal.T, preferred_element_type=jnp.float32)
    score_gradient = (expo * weight_gradient * logit_scale).astype(jnp.bfloat16)
    d_query = jnp.dot(score_gradient, upstream_signal, preferred_element_type=jnp.float32) + direct
    d_frames = jnp.dot(score_gradient.T, query_vectors, preferred_element_type=jnp.float32)
    d_frames = d_frames + jnp.dot(batch_weights.T, context_batch_gradient, preferred_element_type=jnp.float32)
    return (loss_part, d_query, d_frames)

def reference(frames, texts, pair_rec, pair_text, pair_label):

    def per_record(carry, inputs):
        text_grad, loss = carry
        upstream_signal, here = inputs
        valid, slot_text, sign = slot_tables(pair_rec, pair_text, pair_label, here, MOST)
        query_vectors = jnp.take(texts, slot_text, axis=0)

        def per_slot(frame_grad, slot_in):
            one_query, one_valid, one_sign = slot_in

            def active(operands):
                return slot_pass(upstream_signal, operands[0], operands[1], operands[2])

            def silent(operands):
                return (jnp.zeros((), jnp.float32), jnp.zeros((L, D), jnp.float32), jnp.zeros((FRAMES, D), jnp.float32))
            loss_part, d_query, d_frames = lax.cond(one_valid > 0, active, silent, (one_query, one_valid, one_sign))
            return (frame_grad + d_frames, (loss_part, d_query))
        frame_grad, outputs = lax.scan(per_slot, jnp.zeros((FRAMES, D), jnp.float32), (query_vectors, valid.astype(jnp.float32), sign.astype(jnp.float32)))
        losses, d_query = outputs
        text_grad = text_grad.at[slot_text].add(d_query * valid.astype(jnp.float32)[:, None, None])
        return ((text_grad, loss + jnp.sum(losses)), frame_grad.astype(jnp.bfloat16))
    start = (jnp.zeros((TEXTS, L, D), jnp.float32), jnp.zeros((), jnp.float32))
    final, grad_frames = lax.scan(per_record, start, (frames, jnp.arange(RECS, dtype=jnp.int32)))
    text_grad, loss = final
    return (loss, grad_frames, text_grad.astype(jnp.bfloat16))
```

```python
import jax
import jax.numpy as jnp
from jax import lax
from jax.experimental import pallas as pl
from jax.experimental.pallas import tpu as pltpu
from jax.sharding import PartitionSpec as P

EPS = 1e-06
TEMP = 10.0
BIAS = -1.0
LOSS_SCALE = 2048.0

X, Y = 4, 8
RECS = 16
OFFS = (1, 15, 8)
GROUPS = 3
D = 256
BLK = 16
COL = Y * BLK
ROWS = X * COL
TOKENS = 224
FR = 1536
SCALE = D**-0.5
MESH = pl.DeviceIdType.MESH
F32 = jnp.float32
BF16 = jnp.bfloat16

NT = (((1,), (1,)), ((), ()))
NN = (((1,), (0,)), ((), ()))
TN = (((0,), (0,)), ((), ()))


def dot(a, b, dims):
    return lax.dot_general(a, b, dims, preferred_element_type=F32)


def split_row(v, lane, row):
    hi = v.astype(BF16).astype(F32)
    rest = v - hi
    mid = rest.astype(BF16).astype(F32)
    low = rest - mid
    part = jnp.where(lane < 16, hi, jnp.where(lane < 32, mid, low))
    part = jnp.where((lane < 48) & ((lane & 15) == row), part, 0.0)
    return jnp.sum(part, axis=1, keepdims=True)


def kernel(
    rec_ref, text_ref, label_ref, frames_ref, texts_ref,
    loss_ref, gf_ref, gt_ref,
    own, q, w, s_s, m_o, m_i, t_o, t_i, m_t, part0, rsx_o, rsx_i, rsy_o, rsy_i, direct, uy, col_o, col_i, u, ds, dq0,
    dx_o, dx_i, dy_o, dy_i, back_o, back_i, gft, pad, gcos, loss_o, loss_i,
    s_text, r_text, s_st, r_st, s_back, r_back, s_loss, r_loss,
):
    r, f = lax.axis_index("rec"), lax.axis_index("frame")
    x, y = f // Y, f % Y

    def at_y(k):
        return (r, x * Y + lax.rem(y + k, Y))

    def at_x(k):
        return (r, lax.rem(x + k, X) * Y + y)

    def at_r(k):
        return (lax.rem(r + k, RECS), f)

    barrier = pltpu.get_barrier_semaphore()
    for k in range(1, RECS):
        pl.semaphore_signal(barrier, inc=1, device_id=at_r(k), device_id_type=MESH)
    for k in range(1, Y):
        pl.semaphore_signal(barrier, inc=1, device_id=at_y(k), device_id_type=MESH)
    for k in range(1, X):
        pl.semaphore_signal(barrier, inc=1, device_id=at_x(k), device_id_type=MESH)

    pad[...] = jnp.zeros_like(pad)
    pad[0:7, :] = texts_ref[0].astype(F32)
    pad[8:15, :] = texts_ref[1].astype(F32)
    own[...] = pad[...].astype(BF16)

    def count(p, c):
        rec = rec_ref[p, 0]
        text = text_ref[p]
        label = label_ref[p]
        hop = ((text >> 1) - rec) & (RECS - 1)
        mine = (rec == r).astype(jnp.int32)
        out = []
        for g in range(GROUPS):
            for s in range(2):
                hit = mine * (hop == OFFS[g]).astype(jnp.int32) * ((text & 1) == s).astype(jnp.int32)
                out.append(c[len(out)] + hit * label)
                out.append(c[len(out)] + hit * (1 - label))
        return tuple(out)

    counts = lax.fori_loop(0, 32, count, (jnp.int32(0),) * 12)

    pl.semaphore_wait(barrier, RECS - 1 + Y - 1 + X - 1)

    def send(src, dst, ss, rs, to):
        pltpu.make_async_remote_copy(src, dst, ss, rs, device_id=to, device_id_type=MESH).start()

    def wait(ref, sem):
        pltpu.make_async_copy(ref, ref, sem).wait()

    def gather_y(buf, g, st):
        for k in range(1, Y):
            send(buf.at[g, pl.ds(0, BLK)], buf.at[g, pl.ds(k * BLK, BLK)], s_st.at[st, g], r_st.at[st, g], at_y(k))

    def gather_x(buf, g, st):
        for k in range(1, X):
            send(buf.at[g, pl.ds(0, COL)], buf.at[g, pl.ds(k * COL, COL)], s_st.at[st, g], r_st.at[st, g], at_x(k))

    def scatter_x(out, into, g, k, st):
        send(out.at[g, k - 1], into.at[g, k - 1], s_st.at[st, g], r_st.at[st, g], at_x(X - k))

    def scatter_y(out, into, g, st):
        for k in range(1, Y):
            send(out.at[g, pl.ds(k * BLK - BLK, BLK)], into.at[g, pl.ds(k * BLK - BLK, BLK)], s_st.at[st, g], r_st.at[st, g], at_y(Y - k))

    for g in range(GROUPS):
        send(own, q.at[g, pl.ds(0, BLK)], s_text.at[g], r_text.at[g], at_r(RECS - OFFS[g]))

    def stage_a(g, c):
        wait(q.at[g, pl.ds(0, BLK)], r_text.at[g])
        gather_y(q, g, 0)
        return c

    lax.fori_loop(0, GROUPS, stage_a, 0)

    def stage_b(g, c):
        wait(q.at[g, pl.ds(BLK, COL - BLK)], r_st.at[0, g])
        gather_x(q, g, 1)
        return c

    lax.fori_loop(0, GROUPS, stage_b, 0)

    square = (COL, COL)
    diag = lax.broadcasted_iota(jnp.int32, square, 0) == lax.broadcasted_iota(jnp.int32, square, 1)

    def stage_c(g, c):
        def score(k):
            rows = pl.ds(k * COL, COL)
            s = dot(q[g, rows, :], frames_ref[0], NT) * SCALE
            s_s[g, rows, :] = s
            m = jnp.max(s, axis=1, keepdims=True)
            line = jnp.sum(jnp.where(diag, m, 0.0), axis=0, keepdims=True)
            m_o[g, pl.ds(k, 1), :] = line
            m_o[g, pl.ds(k + X, 1), :] = line

        score(0)
        wait(q.at[g, pl.ds(COL, ROWS - COL)], r_st.at[1, g])

        def one(k, c):
            score(k)
            return c

        lax.fori_loop(1, X, one, 0)
        for k in range(1, X):
            send(m_o.at[g], m_i.at[g, k - 1], s_st.at[2, g], r_st.at[2, g], at_x(k))
        return c

    lax.fori_loop(0, GROUPS, stage_c, 0)

    def stage_m(g, c):
        wait(m_i.at[g], r_st.at[2, g])
        top = m_o[g]
        for k in range(1, X):
            top = jnp.maximum(top, pltpu.roll(m_i[g, k - 1], k, 0))
        t_o[g] = top
        for k in range(1, Y):
            send(t_o.at[g], t_i.at[g, k - 1], s_st.at[3, g], r_st.at[3, g], at_y(k))
        return c

    lax.fori_loop(0, GROUPS, stage_m, 0)

    def stage_w(g, c):
        wait(t_i.at[g], r_st.at[3, g])
        top = t_o[g]
        for k in range(1, Y):
            top = jnp.maximum(top, pltpu.roll(t_i[g, k - 1], BLK * k, 1))
        m_t[g] = top

        def context(k):
            rows = pl.ds(k * COL, COL)
            m = jnp.sum(jnp.where(diag, m_t[g, pl.ds(k, 1), :], 0.0), axis=1, keepdims=True)
            wb = jnp.exp(s_s[g, rows, :] - m).astype(BF16)
            w[g, rows, :] = wb
            return dot(wb, frames_ref[0], NN)

        def one(k, c):
            rsx_o[g, k - 1] = context(k)
            scatter_x(rsx_o, rsx_i, g, k, 9)
            return c

        lax.fori_loop(1, X, one, 0)
        part0[g] = context(0)
        return c

    lax.fori_loop(0, GROUPS, stage_w, 0)

    def stage_d(g, c):
        wait(rsx_i.at[g], r_st.at[9, g])
        total = part0[g]
        for k in range(X - 1):
            total = total + rsx_i[g, k]
        part0[g, pl.ds(0, BLK), :] = total[:BLK]
        rsy_o[g] = total[BLK:]
        scatter_y(rsy_o, rsy_i, g, 10)
        return c

    lax.fori_loop(0, GROUPS, stage_d, 0)

    def stage_e(g, c):
        wait(rsy_i.at[g], r_st.at[10, g])
        qf = q[g, pl.ds(0, BLK), :].astype(F32).reshape(1, BLK, D)
        rest = rsy_i[g].reshape(Y - 1, BLK, D)
        ctx = part0[g, pl.ds(0, BLK), :].reshape(1, BLK, D) + jnp.sum(rest, axis=0, keepdims=True)
        lane = lax.broadcasted_iota(jnp.int32, (1, BLK, D), 2)
        row = lax.broadcasted_iota(jnp.int32, (1, BLK, D), 1)
        q_norm = lax.rsqrt(jnp.sum(qf * qf, axis=2, keepdims=True) + EPS)
        c_norm = lax.rsqrt(jnp.sum(ctx * ctx, axis=2, keepdims=True) + EPS)
        q_unit = qf * q_norm
        c_unit = ctx * c_norm
        cos = jnp.sum(q_unit * c_unit, axis=2, keepdims=True)
        d_ctx = (q_unit - cos * c_unit) * c_norm
        direct[g] = ((c_unit - cos * q_unit) * q_norm).reshape(BLK, D)
        d_ctx = jnp.where(row == 15, split_row(cos, lane, row), d_ctx).reshape(BLK, D)
        high = d_ctx.astype(BF16)
        uy[g, 0, 0:BLK, :] = high
        uy[g, 0, BLK:, :] = (d_ctx - high.astype(F32)).astype(BF16)
        for k in range(1, Y):
            send(uy.at[g, 0], uy.at[g, k], s_st.at[4, g], r_st.at[4, g], at_y(k))
        return c

    lax.fori_loop(0, GROUPS, stage_e, 0)

    def stage_f(g, c):
        wait(uy.at[g, pl.ds(1, Y - 1)], r_st.at[4, g])
        sums = jnp.sum(uy[g, :, 0:BLK, :].astype(F32)[:, 15, :128], axis=0, keepdims=True)
        col_o[g] = jnp.broadcast_to(sums, (8, 128))
        for k in range(1, X):
            send(col_o.at[g], col_i.at[g, k - 1], s_st.at[8, g], r_st.at[8, g], at_x(k))
        return c

    lax.fori_loop(0, GROUPS, stage_f, 0)

    loss = jnp.zeros((1, 128), F32)
    for g in range(GROUPS):
        wait(col_i.at[g], r_st.at[8, g])
        sums = col_o[g, 0:1, :] + col_i[g, 0, 0:1, :] + col_i[g, 1, 0:1, :] + col_i[g, 2, 0:1, :]
        lane = lax.broadcasted_iota(jnp.int32, (1, 128), 1)
        for s in range(2):
            pick = (lane < 48) & (((lane >> 3) & 1) == s) & ((lane & 7) < 7)
            score = jnp.sum(jnp.where(pick, sums, 0.0), axis=1, keepdims=True) * (1.0 / TOKENS)
            logit = jnp.broadcast_to(TEMP * score + BIAS, (1, 128))
            yes = counts[4 * g + 2 * s].astype(F32)
            no = counts[4 * g + 2 * s + 1].astype(F32)
            tail = jnp.log1p(jnp.exp(-jnp.abs(logit)))
            loss = loss + yes * (jnp.maximum(-logit, 0.0) + tail) + no * (jnp.maximum(logit, 0.0) + tail)
            pull = yes / (1.0 + jnp.exp(logit)) - no / (1.0 + jnp.exp(-logit))
            gcos[g, pl.ds(8 * s, 8), :] = jnp.broadcast_to(-LOSS_SCALE * TEMP / TOKENS * pull, (8, 128))
        row = lax.broadcasted_iota(jnp.int32, (Y, BLK, 1), 1)
        high = uy[g, :, 0:BLK, :].astype(F32)
        whole = (high + uy[g, :, BLK:, :].astype(F32)) * gcos[g, :, 0:1].reshape(1, BLK, 1)
        u[g, pl.ds(0, COL), :] = jnp.where((row & 7) < 7, whole, 0.0).reshape(COL, D).astype(BF16)
        gather_x(u, g, 5)

    loss_o[...] = jnp.broadcast_to(loss, (8, 128))
    for k in range(1, RECS):
        send(loss_o, loss_i.at[k - 1], s_loss, r_loss, at_r(k))

    for g in range(GROUPS):
        wait(u.at[g, pl.ds(COL, ROWS - COL)], r_st.at[5, g])

        def back(k, g=g):
            rows = pl.ds(k * COL, COL)
            dw = dot(u[g, rows, :], frames_ref[0], NT)
            d = (w[g, rows, :].astype(F32) * dw * SCALE).astype(BF16)
            ds[g, rows, :] = d
            return dot(d, frames_ref[0], NN)

        def one(k, c, g=g, back=back):
            dx_o[g, k - 1] = back(k).astype(BF16)
            scatter_x(dx_o, dx_i, g, k, 6)
            return c

        lax.fori_loop(1, X, one, 0)
        dq0[g] = back(0)

    def frame_grad(g):
        def tile(n, c):
            cols = pl.ds(pl.multiple_of(n * 512, 512), 512)
            acc = dot(q[g], ds[g, :, cols], TN) + dot(u[g], w[g, :, cols], TN)
            if g:
                acc = acc + gft[:, cols]
            if g < GROUPS - 1:
                gft[:, cols] = acc
            else:
                gf_ref[0, cols, :] = acc.T.astype(BF16)
            return c

        lax.fori_loop(0, FR // 512, tile, 0)

    def stage_h(g):
        wait(dx_i.at[g], r_st.at[6, g])
        total = dq0[g]
        for k in range(X - 1):
            total = total + dx_i[g, k].astype(F32)
        dq0[g] = total
        dy_o[g] = total[BLK:].astype(BF16)
        scatter_y(dy_o, dy_i, g, 7)

    def stage_i(g):
        wait(dy_i.at[g], r_st.at[7, g])
        total = dq0[g, pl.ds(0, BLK), :] + direct[g] * gcos[g, :, 0:1]
        total = total + jnp.sum(dy_i[g].astype(F32).reshape(Y - 1, BLK, D), axis=0)
        back_o[g] = total.astype(BF16)
        send(back_o.at[g], back_i.at[g], s_back.at[g], r_back.at[g], at_r(OFFS[g]))

    stage_h(0)
    stage_h(1)
    frame_grad(0)
    stage_h(2)
    stage_i(0)
    stage_i(1)
    frame_grad(1)
    stage_i(2)
    frame_grad(2)

    wait(loss_i, r_loss)
    loss_ref[0, 0] = jnp.sum(loss + jnp.sum(loss_i[:, 0, :], axis=0, keepdims=True)) * (1.0 / 128)

    total = None
    for g in range(GROUPS):
        wait(back_i.at[g], r_back.at[g])
        term = back_i[g].astype(F32)
        total = term if total is None else total + term
    gt_ref[0] = total[0:7].astype(BF16)
    gt_ref[1] = total[8:15].astype(BF16)

    for g in range(GROUPS):
        wait(own, s_text.at[g])
        wait(back_o.at[g], s_back.at[g])
        for st, ref in ((0, dy_i), (1, dx_i), (2, m_i), (3, t_i), (5, dx_i), (6, dx_i), (7, dy_i), (8, col_i), (9, rsx_i), (10, rsy_i)):
            wait(ref.at[g], s_st.at[st, g])
        wait(uy.at[g, pl.ds(1, Y - 1)], s_st.at[4, g])
    wait(loss_i, s_loss)


def body(frames, texts, pair_rec, pair_text, pair_label):
    vmem = pl.BlockSpec(memory_space=pltpu.VMEM)
    smem = pl.BlockSpec(memory_space=pltpu.SMEM)
    dma = pltpu.SemaphoreType.DMA
    v = pltpu.VMEM
    loss, gf, gt = pl.pallas_call(
        kernel,
        out_shape=(
            jax.ShapeDtypeStruct((1, 1), F32),
            jax.ShapeDtypeStruct((1, FR, D), BF16),
            jax.ShapeDtypeStruct((2, 7, D), BF16),
        ),
        in_specs=[smem, smem, smem, vmem, vmem],
        out_specs=(smem, vmem, vmem),
        scratch_shapes=[
            v((BLK, D), BF16),
            v((GROUPS, ROWS, D), BF16),
            v((GROUPS, ROWS, FR), BF16),
            v((GROUPS, ROWS, FR), F32),
            v((GROUPS, 8, 128), F32),
            v((GROUPS, X - 1, 8, 128), F32),
            v((GROUPS, 8, 128), F32),
            v((GROUPS, Y - 1, 8, 128), F32),
            v((GROUPS, 8, 128), F32),
            v((GROUPS, COL, D), F32),
            v((GROUPS, X - 1, COL, D), F32),
            v((GROUPS, X - 1, COL, D), F32),
            v((GROUPS, COL - BLK, D), F32),
            v((GROUPS, COL - BLK, D), F32),
            v((GROUPS, BLK, D), F32),
            v((GROUPS, Y, 2 * BLK, D), BF16),
            v((GROUPS, 8, 128), F32),
            v((GROUPS, X - 1, 8, 128), F32),
            v((GROUPS, ROWS, D), BF16),
            v((GROUPS, ROWS, FR), BF16),
            v((GROUPS, COL, D), F32),
            v((GROUPS, X - 1, COL, D), BF16),
            v((GROUPS, X - 1, COL, D), BF16),
            v((GROUPS, COL - BLK, D), BF16),
            v((GROUPS, COL - BLK, D), BF16),
            v((GROUPS, BLK, D), BF16),
            v((GROUPS, BLK, D), BF16),
            v((D, FR), F32),
            v((BLK, D), F32),
            v((GROUPS, BLK, 128), F32),
            v((8, 128), F32),
            v((RECS - 1, 8, 128), F32),
            dma((GROUPS,)), dma((GROUPS,)),
            dma((11, GROUPS)), dma((11, GROUPS)),
            dma((GROUPS,)), dma((GROUPS,)),
            dma, dma,
        ],
        compiler_params=pltpu.CompilerParams(
            collective_id=0, has_side_effects=True, vmem_limit_bytes=48 << 20
        ),
        cost_estimate=pl.CostEstimate(flops=7_300_000_000, bytes_accessed=1_700_000, transcendentals=2_400_000),
    )(pair_rec, pair_text, pair_label, frames, texts)
    return (loss.reshape(()), gf, gt)


def solution(mesh):
    return jax.shard_map(
        body,
        mesh=mesh,
        in_specs=(P("rec", "frame", None), P("rec", "frame", None), P(), P(), P()),
        out_specs=(P(), P("rec", "frame", None), P("rec", "frame", None)),
        check_vma=False,
    )
```

```python
import jax
import jax.numpy as jnp
from jax import lax
from jax.experimental import pallas as pl
from jax.experimental.pallas import tpu as pltpu
from jax.sharding import PartitionSpec as P

EPS = 1e-06
TEMP = 10.0
BIAS = -1.0
LOSS_SCALE = 2048.0

X, Y = 4, 8
RECS = 16
OFFS = (1, 15, 8)
GROUPS = 3
D = 256
BLK = 16
HALF = Y * BLK // 2
COL = Y * BLK
ROWS = X * COL
TOKENS = 224
FR = 1536
SCALE = D**-0.5
MESH = pl.DeviceIdType.MESH
F32 = jnp.float32
BF16 = jnp.bfloat16

NN = (((1,), (0,)), ((), ()))
TN = (((0,), (0,)), ((), ()))


def dot(a, b, dims):
    return lax.dot_general(a, b, dims, preferred_element_type=F32)


def split_row(v, lane, row):
    hi = v.astype(BF16).astype(F32)
    rest = v - hi
    mid = rest.astype(BF16).astype(F32)
    low = rest - mid
    part = jnp.where(lane < 16, hi, jnp.where(lane < 32, mid, low))
    part = jnp.where((lane < 48) & ((lane & 15) == row), part, 0.0)
    return jnp.sum(part, axis=1, keepdims=True)


def kernel(
    rec_ref, text_ref, label_ref, frames_hbm, texts_ref,
    loss_ref, gf_ref, gt_ref,
    frames_ref, turned, own, q, w, s_s, m_o, m_i, t_o, t_i, m_t, part0, rsx_o, rsx_i, rsh, rsh_i, rsy_o, rsy_i, direct, uy, col_o, col_i, u, ds, dq0,
    dx_o, dx_i, dy_o, dy_i, back_o, back_i, gft, pad, gcos, loss_o, loss_i,
    s_frames, s_text, r_text, s_st, r_st, r_ax, r_h, s_back, r_back, s_loss, r_loss,
):
    r, f = lax.axis_index("rec"), lax.axis_index("frame")
    x, y = f // Y, f % Y

    def at_y(k):
        return (r, x * Y + lax.rem(y + k, Y))

    def at_x(k):
        return (r, lax.rem(x + k, X) * Y + y)

    def at_r(k):
        return (lax.rem(r + k, RECS), f)

    load = pltpu.make_async_copy(frames_hbm.at[0], frames_ref, s_frames)
    load.start()
    barrier = pltpu.get_barrier_semaphore()
    for k in range(1, RECS):
        pl.semaphore_signal(barrier, inc=1, device_id=at_r(k), device_id_type=MESH)
    for k in range(1, Y):
        pl.semaphore_signal(barrier, inc=1, device_id=at_y(k), device_id_type=MESH)
    for k in range(1, X):
        pl.semaphore_signal(barrier, inc=1, device_id=at_x(k), device_id_type=MESH)

    pad[...] = jnp.zeros_like(pad)
    pad[0:7, :] = texts_ref[0].astype(F32)
    pad[8:15, :] = texts_ref[1].astype(F32)
    own[...] = pad[...].astype(BF16)

    pl.semaphore_wait(barrier, RECS - 1 + Y - 1 + X - 1)

    def send(src, dst, ss, rs, to):
        pltpu.make_async_remote_copy(src, dst, ss, rs, device_id=to, device_id_type=MESH).start()

    def wait(ref, sem):
        pltpu.make_async_copy(ref, ref, sem).wait()

    def gather_y(buf, g, st):
        for k in range(1, Y):
            send(buf.at[g, pl.ds(0, BLK)], buf.at[g, pl.ds(k * BLK, BLK)], s_st.at[st, g], r_st.at[st, g], at_y(k))

    def gather_x(buf, g, st, i):
        send(buf.at[g, pl.ds(0, COL)], buf.at[g, pl.ds(COL, COL)], s_st.at[st, g], r_ax.at[i, g, 0], at_x(1))
        send(buf.at[g, pl.ds(0, COL)], buf.at[g, pl.ds(3 * COL, COL)], s_st.at[st, g], r_ax.at[i, g, 1], at_x(3))

    def forward_x(buf, g, st, i):
        near, far, half = pl.ds(COL, HALF), pl.ds(3 * COL + HALF, HALF), 2 * COL + HALF
        wait(buf.at[g, pl.ds(COL, COL)], r_ax.at[i, g, 0])
        send(buf.at[g, near], buf.at[g, pl.ds(2 * COL, HALF)], s_st.at[st, g], r_ax.at[i, g, 2], at_x(1))
        wait(buf.at[g, pl.ds(3 * COL, COL)], r_ax.at[i, g, 1])
        send(buf.at[g, far], buf.at[g, pl.ds(half, HALF)], s_st.at[st, g], r_ax.at[i, g, 2], at_x(3))

    def scatter_x(out, into, g, k, st):
        send(out.at[g, k - 1], into.at[g, k - 1], s_st.at[st, g], r_st.at[st, g], at_x(X - k))

    def scatter_far(out, halves, g, st, i):
        send(out.at[g, 2, pl.ds(0, HALF)], halves.at[g, 0], s_st.at[st, g], r_h.at[i, g, 0], at_x(3))
        send(out.at[g, 2, pl.ds(HALF, HALF)], halves.at[g, 1], s_st.at[st, g], r_h.at[i, g, 1], at_x(1))

    def scatter_first(out, into, g, st, side):
        rows = pl.ds(HALF - HALF * side, HALF)
        send(out.at[g, side, rows], into.at[g, side, rows], s_st.at[st, g], r_st.at[st, g], at_x(3 - 2 * side))

    def scatter_last(out, into, halves, mine, g, st, i):
        for side in range(2):
            rows = pl.ds(HALF * side, HALF)
            wait(halves.at[g, side], r_h.at[i, g, side])
            out[g, side, rows, :] = (mine[g, side] + halves[g, side].astype(F32)).astype(out.dtype)
            send(out.at[g, side, rows], into.at[g, side, rows], s_st.at[st, g], r_st.at[st, g], at_x(3 - 2 * side))

    def scatter_y(out, into, g, st):
        for k in range(1, Y):
            send(out.at[g, pl.ds(k * BLK - BLK, BLK)], into.at[g, pl.ds(k * BLK - BLK, BLK)], s_st.at[st, g], r_st.at[st, g], at_y(Y - k))

    for g in range(GROUPS):
        send(own, q.at[g, pl.ds(0, BLK)], s_text.at[g], r_text.at[g], at_r(RECS - OFFS[g]))

    def count(p, c):
        rec = rec_ref[p, 0]
        text = text_ref[p]
        label = label_ref[p]
        hop = ((text >> 1) - rec) & (RECS - 1)
        mine = (rec == r).astype(jnp.int32)
        out = []
        for g in range(GROUPS):
            for s in range(2):
                hit = mine * (hop == OFFS[g]).astype(jnp.int32) * ((text & 1) == s).astype(jnp.int32)
                out.append(c[len(out)] + hit * label)
                out.append(c[len(out)] + hit * (1 - label))
        return tuple(out)

    counts = lax.fori_loop(0, 32, count, (jnp.int32(0),) * 12)

    load.wait()

    def turn(n, c):
        at = pl.ds(pl.multiple_of(n * 256, 256), 256)
        turned[:, at] = frames_ref[at, :].T
        return c

    lax.fori_loop(0, FR // 256, turn, 0)

    def stage_a(g, c):
        wait(q.at[g, pl.ds(0, BLK)], r_text.at[g])
        gather_y(q, g, 0)
        return c

    lax.fori_loop(0, GROUPS, stage_a, 0)

    def stage_b(g, c):
        wait(q.at[g, pl.ds(BLK, COL - BLK)], r_st.at[0, g])
        gather_x(q, g, 1, 0)
        return c

    lax.fori_loop(0, GROUPS, stage_b, 0)

    square = (COL, COL)
    diag = lax.broadcasted_iota(jnp.int32, square, 0) == lax.broadcasted_iota(jnp.int32, square, 1)

    def stage_c(g, c):
        def score(k):
            rows = pl.ds(k * COL, COL)
            s = dot(q[g, rows, :], turned[...], NN) * SCALE
            s_s[g, rows, :] = s
            m = jnp.max(s, axis=1, keepdims=True)
            line = jnp.sum(jnp.where(diag, m, 0.0), axis=0, keepdims=True)
            m_o[g, pl.ds(k, 1), :] = line
            m_o[g, pl.ds(k + X, 1), :] = line

        @pl.when(g < GROUPS - 1)
        def _():
            forward_x(q, g + 1, 1, 0)

        def one(k, c):
            score(lax.rem(k, X))
            return c

        lax.fori_loop(3, 6, one, 0)
        wait(q.at[g, pl.ds(2 * COL, COL)], r_ax.at[0, g, 2])
        score(2)
        for k in range(1, X):
            send(m_o.at[g], m_i.at[g, k - 1], s_st.at[2, g], r_st.at[2, g], at_x(k))
        return c

    forward_x(q, 0, 1, 0)
    lax.fori_loop(0, GROUPS, stage_c, 0)

    def stage_m(g, c):
        wait(m_i.at[g], r_st.at[2, g])
        top = m_o[g]
        for k in range(1, X):
            top = jnp.maximum(top, pltpu.roll(m_i[g, k - 1], k, 0))
        t_o[g] = top
        for k in range(1, Y):
            send(t_o.at[g], t_i.at[g, k - 1], s_st.at[3, g], r_st.at[3, g], at_y(k))
        return c

    lax.fori_loop(0, GROUPS, stage_m, 0)

    def stage_w(g, c):
        wait(t_i.at[g], r_st.at[3, g])
        top = t_o[g]
        for k in range(1, Y):
            top = jnp.maximum(top, pltpu.roll(t_i[g, k - 1], BLK * k, 1))
        m_t[g] = top

        def context(k):
            rows = pl.ds(k * COL, COL)
            m = jnp.sum(jnp.where(diag, m_t[g, pl.ds(k, 1), :], 0.0), axis=1, keepdims=True)
            wb = jnp.exp(s_s[g, rows, :] - m).astype(BF16)
            w[g, rows, :] = wb
            return dot(wb, frames_ref[...], NN)

        rsx_o[g, 2] = context(2)
        scatter_far(rsx_o, rsh_i, g, 9, 0)

        def one(side, c):
            value = context(1 + 2 * side)
            rsx_o[g, side] = value
            rsh[g, side] = rsx_o[g, side, pl.ds(HALF * side, HALF), :]
            scatter_first(rsx_o, rsx_i, g, 9, side)
            return c

        lax.fori_loop(0, 2, one, 0)
        part0[g] = context(0)

        @pl.when(g > 0)
        def _():
            scatter_last(rsx_o, rsx_i, rsh_i, rsh, g - 1, 9, 0)

        return c

    lax.fori_loop(0, GROUPS, stage_w, 0)
    scatter_last(rsx_o, rsx_i, rsh_i, rsh, GROUPS - 1, 9, 0)

    def stage_d(g, c):
        wait(rsx_i.at[g], r_st.at[9, g])
        total = part0[g] + rsx_i[g, 0] + rsx_i[g, 1]
        part0[g, pl.ds(0, BLK), :] = total[:BLK]
        rsy_o[g] = total[BLK:]
        scatter_y(rsy_o, rsy_i, g, 10)
        return c

    lax.fori_loop(0, GROUPS, stage_d, 0)

    def stage_e(g, c):
        wait(rsy_i.at[g], r_st.at[10, g])
        qf = q[g, pl.ds(0, BLK), :].astype(F32).reshape(1, BLK, D)
        rest = rsy_i[g].reshape(Y - 1, BLK, D)
        ctx = part0[g, pl.ds(0, BLK), :].reshape(1, BLK, D) + jnp.sum(rest, axis=0, keepdims=True)
        lane = lax.broadcasted_iota(jnp.int32, (1, BLK, D), 2)
        row = lax.broadcasted_iota(jnp.int32, (1, BLK, D), 1)
        q_norm = lax.rsqrt(jnp.sum(qf * qf, axis=2, keepdims=True) + EPS)
        c_norm = lax.rsqrt(jnp.sum(ctx * ctx, axis=2, keepdims=True) + EPS)
        q_unit = qf * q_norm
        c_unit = ctx * c_norm
        cos = jnp.sum(q_unit * c_unit, axis=2, keepdims=True)
        d_ctx = (q_unit - cos * c_unit) * c_norm
        direct[g] = ((c_unit - cos * q_unit) * q_norm).reshape(BLK, D)
        d_ctx = jnp.where(row == 15, split_row(cos, lane, row), d_ctx).reshape(BLK, D)
        high = d_ctx.astype(BF16)
        uy[g, 0, 0:BLK, :] = high
        uy[g, 0, BLK:, :] = (d_ctx - high.astype(F32)).astype(BF16)
        for k in range(1, Y):
            send(uy.at[g, 0], uy.at[g, k], s_st.at[4, g], r_st.at[4, g], at_y(k))
        return c

    lax.fori_loop(0, GROUPS, stage_e, 0)

    def stage_f(g, c):
        wait(uy.at[g, pl.ds(1, Y - 1)], r_st.at[4, g])
        sums = jnp.sum(uy[g, :, 0:BLK, :].astype(F32)[:, 15, :128], axis=0, keepdims=True)
        col_o[g] = jnp.broadcast_to(sums, (8, 128))
        for k in range(1, X):
            send(col_o.at[g], col_i.at[g, k - 1], s_st.at[8, g], r_st.at[8, g], at_x(k))
        return c

    lax.fori_loop(0, GROUPS, stage_f, 0)

    loss = jnp.zeros((1, 128), F32)
    for g in range(GROUPS):
        wait(col_i.at[g], r_st.at[8, g])
        sums = col_o[g, 0:1, :] + col_i[g, 0, 0:1, :] + col_i[g, 1, 0:1, :] + col_i[g, 2, 0:1, :]
        lane = lax.broadcasted_iota(jnp.int32, (1, 128), 1)
        for s in range(2):
            pick = (lane < 48) & (((lane >> 3) & 1) == s) & ((lane & 7) < 7)
            score = jnp.sum(jnp.where(pick, sums, 0.0), axis=1, keepdims=True) * (1.0 / TOKENS)
            logit = jnp.broadcast_to(TEMP * score + BIAS, (1, 128))
            yes = counts[4 * g + 2 * s].astype(F32)
            no = counts[4 * g + 2 * s + 1].astype(F32)
            tail = jnp.log1p(jnp.exp(-jnp.abs(logit)))
            loss = loss + yes * (jnp.maximum(-logit, 0.0) + tail) + no * (jnp.maximum(logit, 0.0) + tail)
            pull = yes / (1.0 + jnp.exp(logit)) - no / (1.0 + jnp.exp(-logit))
            gcos[g, pl.ds(8 * s, 8), :] = jnp.broadcast_to(-LOSS_SCALE * TEMP / TOKENS * pull, (8, 128))
        row = lax.broadcasted_iota(jnp.int32, (Y, BLK, 1), 1)
        high = uy[g, :, 0:BLK, :].astype(F32)
        whole = (high + uy[g, :, BLK:, :].astype(F32)) * gcos[g, :, 0:1].reshape(1, BLK, 1)
        u[g, pl.ds(0, COL), :] = jnp.where((row & 7) < 7, whole, 0.0).reshape(COL, D).astype(BF16)
        gather_x(u, g, 5, 1)

    loss_o[...] = jnp.broadcast_to(loss, (8, 128))
    for k in range(1, RECS):
        send(loss_o, loss_i.at[k - 1], s_loss, r_loss, at_r(k))

    forward_x(u, 0, 5, 1)

    def stage_g(g, c):
        @pl.when(g < GROUPS - 1)
        def _():
            forward_x(u, g + 1, 5, 1)

        def back(k):
            rows = pl.ds(k * COL, COL)
            dw = dot(u[g, rows, :], turned[...], NN)
            d = (w[g, rows, :].astype(F32) * dw * SCALE).astype(BF16)
            ds[g, rows, :] = d
            return dot(d, frames_ref[...], NN)

        wait(u.at[g, pl.ds(2 * COL, COL)], r_ax.at[1, g, 2])

        def one(k, c):
            dx_o[g, k - 1] = back(k).astype(BF16)
            scatter_x(dx_o, dx_i, g, k, 6)
            return c

        lax.fori_loop(1, X, one, 0)
        dq0[g] = back(0)
        return c

    lax.fori_loop(0, GROUPS, stage_g, 0)

    def frame_grad(g):
        def tile(n, c):
            cols = pl.ds(pl.multiple_of(n * 512, 512), 512)
            acc = dot(q[g], ds[g, :, cols], TN) + dot(u[g], w[g, :, cols], TN)
            if g:
                acc = acc + gft[:, cols]
            if g < GROUPS - 1:
                gft[:, cols] = acc
            else:
                gf_ref[0, cols, :] = acc.T.astype(BF16)
            return c

        lax.fori_loop(0, FR // 512, tile, 0)

    def stage_h(g):
        wait(dx_i.at[g], r_st.at[6, g])
        total = dq0[g]
        for k in range(X - 1):
            total = total + dx_i[g, k].astype(F32)
        dq0[g] = total
        dy_o[g] = total[BLK:].astype(BF16)
        scatter_y(dy_o, dy_i, g, 7)

    def stage_i(g):
        wait(dy_i.at[g], r_st.at[7, g])
        total = dq0[g, pl.ds(0, BLK), :] + direct[g] * gcos[g, :, 0:1]
        total = total + jnp.sum(dy_i[g].astype(F32).reshape(Y - 1, BLK, D), axis=0)
        back_o[g] = total.astype(BF16)
        send(back_o.at[g], back_i.at[g], s_back.at[g], r_back.at[g], at_r(OFFS[g]))

    stage_h(0)
    stage_h(1)
    frame_grad(0)
    stage_h(2)
    stage_i(0)
    stage_i(1)
    frame_grad(1)
    stage_i(2)
    frame_grad(2)

    wait(loss_i, r_loss)
    loss_ref[0, 0] = jnp.sum(loss + jnp.sum(loss_i[:, 0, :], axis=0, keepdims=True)) * (1.0 / 128)

    total = None
    for g in range(GROUPS):
        wait(back_i.at[g], r_back.at[g])
        term = back_i[g].astype(F32)
        total = term if total is None else total + term
    gt_ref[0] = total[0:7].astype(BF16)
    gt_ref[1] = total[8:15].astype(BF16)

    for g in range(GROUPS):
        wait(own, s_text.at[g])
        wait(back_o.at[g], s_back.at[g])
        for st, ref in ((0, dy_i), (1, dx_o), (2, m_i), (3, t_i), (5, dx_o), (6, dx_o), (7, dy_i), (8, col_i), (9, rsx_o), (10, rsy_i)):
            wait(ref.at[g], s_st.at[st, g])
        wait(uy.at[g, pl.ds(1, Y - 1)], s_st.at[4, g])
    wait(loss_i, s_loss)


def body(frames, texts, pair_rec, pair_text, pair_label):
    vmem = pl.BlockSpec(memory_space=pltpu.VMEM)
    smem = pl.BlockSpec(memory_space=pltpu.SMEM)
    dma = pltpu.SemaphoreType.DMA
    v = pltpu.VMEM
    loss, gf, gt = pl.pallas_call(
        kernel,
        out_shape=(
            jax.ShapeDtypeStruct((1, 1), F32),
            jax.ShapeDtypeStruct((1, FR, D), BF16),
            jax.ShapeDtypeStruct((2, 7, D), BF16),
        ),
        in_specs=[smem, smem, smem, pl.BlockSpec(memory_space=pl.ANY), vmem],
        out_specs=(smem, vmem, vmem),
        scratch_shapes=[
            v((FR, D), BF16),
            v((D, FR), BF16),
            v((BLK, D), BF16),
            v((GROUPS, ROWS, D), BF16),
            v((GROUPS, ROWS, FR), BF16),
            v((GROUPS, ROWS, FR), F32),
            v((GROUPS, 8, 128), F32),
            v((GROUPS, X - 1, 8, 128), F32),
            v((GROUPS, 8, 128), F32),
            v((GROUPS, Y - 1, 8, 128), F32),
            v((GROUPS, 8, 128), F32),
            v((GROUPS, COL, D), F32),
            v((GROUPS, X - 1, COL, D), F32),
            v((GROUPS, 2, COL, D), F32),
            v((GROUPS, 2, HALF, D), F32),
            v((GROUPS, 2, HALF, D), F32),
            v((GROUPS, COL - BLK, D), F32),
            v((GROUPS, COL - BLK, D), F32),
            v((GROUPS, BLK, D), F32),
            v((GROUPS, Y, 2 * BLK, D), BF16),
            v((GROUPS, 8, 128), F32),
            v((GROUPS, X - 1, 8, 128), F32),
            v((GROUPS, ROWS, D), BF16),
            v((GROUPS, ROWS, FR), BF16),
            v((GROUPS, COL, D), F32),
            v((GROUPS, X - 1, COL, D), BF16),
            v((GROUPS, X - 1, COL, D), BF16),
            v((GROUPS, COL - BLK, D), BF16),
            v((GROUPS, COL - BLK, D), BF16),
            v((GROUPS, BLK, D), BF16),
            v((GROUPS, BLK, D), BF16),
            v((D, FR), F32),
            v((BLK, D), F32),
            v((GROUPS, BLK, 128), F32),
            v((8, 128), F32),
            v((RECS - 1, 8, 128), F32),
            dma,
            dma((GROUPS,)), dma((GROUPS,)),
            dma((11, GROUPS)), dma((11, GROUPS)),
            dma((2, GROUPS, 3)), dma((1, GROUPS, 2)),
            dma((GROUPS,)), dma((GROUPS,)),
            dma, dma,
        ],
        compiler_params=pltpu.CompilerParams(
            collective_id=0, has_side_effects=True, vmem_limit_bytes=48 << 20
        ),
        cost_estimate=pl.CostEstimate(flops=7_300_000_000, bytes_accessed=1_700_000, transcendentals=2_400_000),
    )(pair_rec, pair_text, pair_label, frames, texts)
    return (loss.reshape(()), gf, gt)


def solution(mesh):
    return jax.shard_map(
        body,
        mesh=mesh,
        in_specs=(P("rec", "frame", None), P("rec", "frame", None), P(), P(), P()),
        out_specs=(P(), P("rec", "frame", None), P("rec", "frame", None)),
        check_vma=False,
    )
```

```python
import functools

import jax
import jax.numpy as jnp
from jax import lax
from jax.experimental import pallas as pl
from jax.experimental.pallas import tpu as pltpu
from jax.sharding import PartitionSpec as P

EPS = 1e-06
TEMP = 10.0
BIAS = -1.0
LOSS_SCALE = 2048.0

X, Y = 4, 8
RECS = 16
OFFS = (1, 15, 8)
OWNERS = 3
D = 256
BLK = 16
HALF = Y * BLK // 2
COL = Y * BLK
ROWS = X * COL
TOKENS = 224
FR = 1536
SCALE = D**-0.5
MESH = pl.DeviceIdType.MESH
F32 = jnp.float32
BF16 = jnp.bfloat16

NN = (((1,), (0,)), ((), ()))
TN = (((0,), (0,)), ((), ()))


def dot(a, b, dims):
    return lax.dot_general(a, b, dims, preferred_element_type=F32)


def split_row(v, lane, row):
    hi = v.astype(BF16).astype(F32)
    rest = v - hi
    mid = rest.astype(BF16).astype(F32)
    low = rest - mid
    part = jnp.where(lane < 16, hi, jnp.where(lane < 32, mid, low))
    part = jnp.where((lane < 48) & ((lane & 15) == row), part, 0.0)
    return jnp.sum(part, axis=1, keepdims=True)


def kernel(
    GROUPS,
    rec_ref, text_ref, label_ref, frames_hbm, texts_ref,
    loss_ref, gf_ref, gt_ref,
    frames_ref, turned, own, texts_i, slots, q, w, s_s, m_o, m_i, t_o, t_i, m_t, part0, rsx_o, rsx_i, rsh, rsh_i, rsy_o, rsy_i, direct, uy, col_o, col_i, u, ds, dq0,
    dx_o, dx_i, dy_o, dy_i, back_o, back_i, gft, pad, gcos, loss_o, loss_i,
    s_frames, s_text, r_text, s_st, r_st, r_ax, r_h, s_back, r_back, s_loss, r_loss,
):
    r, f = lax.axis_index("rec"), lax.axis_index("frame")
    x, y = f // Y, f % Y

    def at_y(k):
        return (r, x * Y + lax.rem(y + k, Y))

    def at_x(k):
        return (r, lax.rem(x + k, X) * Y + y)

    def at_r(k):
        return (lax.rem(r + k, RECS), f)

    load = pltpu.make_async_copy(frames_hbm.at[0], frames_ref, s_frames)
    load.start()
    barrier = pltpu.get_barrier_semaphore()
    for k in range(1, RECS):
        pl.semaphore_signal(barrier, inc=1, device_id=at_r(k), device_id_type=MESH)
    for k in range(1, Y):
        pl.semaphore_signal(barrier, inc=1, device_id=at_y(k), device_id_type=MESH)
    for k in range(1, X):
        pl.semaphore_signal(barrier, inc=1, device_id=at_x(k), device_id_type=MESH)

    pad[...] = jnp.zeros_like(pad)
    pad[0:7, :] = texts_ref[0].astype(F32)
    pad[8:15, :] = texts_ref[1].astype(F32)
    own[...] = pad[...].astype(BF16)

    pl.semaphore_wait(barrier, RECS - 1 + Y - 1 + X - 1)

    def send(src, dst, ss, rs, to):
        pltpu.make_async_remote_copy(src, dst, ss, rs, device_id=to, device_id_type=MESH).start()

    def wait(ref, sem):
        pltpu.make_async_copy(ref, ref, sem).wait()

    def gather_y(buf, g, st):
        for k in range(1, Y):
            send(buf.at[g, pl.ds(0, BLK)], buf.at[g, pl.ds(k * BLK, BLK)], s_st.at[st, g], r_st.at[st, g], at_y(k))

    def gather_x(buf, g, st, i):
        send(buf.at[g, pl.ds(0, COL)], buf.at[g, pl.ds(COL, COL)], s_st.at[st, g], r_ax.at[i, g, 0], at_x(1))
        send(buf.at[g, pl.ds(0, COL)], buf.at[g, pl.ds(3 * COL, COL)], s_st.at[st, g], r_ax.at[i, g, 1], at_x(3))

    def forward_x(buf, g, st, i):
        near, far, half = pl.ds(COL, HALF), pl.ds(3 * COL + HALF, HALF), 2 * COL + HALF
        wait(buf.at[g, pl.ds(COL, COL)], r_ax.at[i, g, 0])
        send(buf.at[g, near], buf.at[g, pl.ds(2 * COL, HALF)], s_st.at[st, g], r_ax.at[i, g, 2], at_x(1))
        wait(buf.at[g, pl.ds(3 * COL, COL)], r_ax.at[i, g, 1])
        send(buf.at[g, far], buf.at[g, pl.ds(half, HALF)], s_st.at[st, g], r_ax.at[i, g, 2], at_x(3))

    def scatter_x(out, into, g, k, st):
        send(out.at[g, k - 1], into.at[g, k - 1], s_st.at[st, g], r_st.at[st, g], at_x(X - k))

    def scatter_far(out, halves, g, st, i):
        send(out.at[g, 2, pl.ds(0, HALF)], halves.at[g, 0], s_st.at[st, g], r_h.at[i, g, 0], at_x(3))
        send(out.at[g, 2, pl.ds(HALF, HALF)], halves.at[g, 1], s_st.at[st, g], r_h.at[i, g, 1], at_x(1))

    def scatter_first(out, into, g, st, side):
        rows = pl.ds(HALF - HALF * side, HALF)
        send(out.at[g, side, rows], into.at[g, side, rows], s_st.at[st, g], r_st.at[st, g], at_x(3 - 2 * side))

    def scatter_last(out, into, halves, mine, g, st, i):
        for side in range(2):
            rows = pl.ds(HALF * side, HALF)
            wait(halves.at[g, side], r_h.at[i, g, side])
            out[g, side, rows, :] = (mine[g, side] + halves[g, side].astype(F32)).astype(out.dtype)
            send(out.at[g, side, rows], into.at[g, side, rows], s_st.at[st, g], r_st.at[st, g], at_x(3 - 2 * side))

    def scatter_y(out, into, g, st):
        for k in range(1, Y):
            send(out.at[g, pl.ds(k * BLK - BLK, BLK)], into.at[g, pl.ds(k * BLK - BLK, BLK)], s_st.at[st, g], r_st.at[st, g], at_y(Y - k))

    for g in range(OWNERS):
        send(own, texts_i.at[g], s_text.at[g], r_text.at[g], at_r(RECS - OFFS[g]))

    def count(p, c):
        rec = rec_ref[p, 0]
        text = text_ref[p]
        label = label_ref[p]
        hop = ((text >> 1) - rec) & (RECS - 1)
        mine = (rec == r).astype(jnp.int32)
        out = []
        for g in range(OWNERS):
            for s in range(2):
                hit = mine * (hop == OFFS[g]).astype(jnp.int32) * ((text & 1) == s).astype(jnp.int32)
                out.append(c[len(out)] + hit * label)
                out.append(c[len(out)] + hit * (1 - label))
        return tuple(out)

    counts = lax.fori_loop(0, 32, count, (jnp.int32(0),) * 12)

    picks, taken = [], jnp.int32(0)
    for t in range(2 * OWNERS):
        named = (counts[2 * t] + counts[2 * t + 1] > 0).astype(jnp.int32)
        picks.append([(named * (taken == j).astype(jnp.int32)).astype(F32) for j in range(2 * GROUPS)])
        taken = taken + named
    slot_yes = [sum(picks[t][j] * counts[2 * t].astype(F32) for t in range(2 * OWNERS)) for j in range(2 * GROUPS)]
    slot_no = [sum(picks[t][j] * counts[2 * t + 1].astype(F32) for t in range(2 * OWNERS)) for j in range(2 * GROUPS)]

    load.wait()

    def turn(n, c):
        at = pl.ds(pl.multiple_of(n * 256, 256), 256)
        turned[:, at] = frames_ref[at, :].T
        return c

    lax.fori_loop(0, FR // 256, turn, 0)

    texts = []
    for g in range(OWNERS):
        wait(texts_i.at[g], r_text.at[g])
        both = texts_i[g].astype(F32)
        texts += [both[:8], both[8:]]
    for g in range(GROUPS):
        mine = [sum(picks[t][2 * g + s] * texts[t] for t in range(2 * OWNERS)) for s in range(2)]
        q[g, pl.ds(0, BLK), :] = jnp.concatenate(mine, axis=0).astype(BF16)
        gather_y(q, g, 0)

    def stage_b(g, c):
        wait(q.at[g, pl.ds(BLK, COL - BLK)], r_st.at[0, g])
        gather_x(q, g, 1, 0)
        return c

    lax.fori_loop(0, GROUPS, stage_b, 0)

    square = (COL, COL)
    diag = lax.broadcasted_iota(jnp.int32, square, 0) == lax.broadcasted_iota(jnp.int32, square, 1)

    def stage_c(g, c):
        def score(k):
            rows = pl.ds(k * COL, COL)
            s = dot(q[g, rows, :], turned[...], NN) * SCALE
            s_s[g, rows, :] = s
            m = jnp.max(s, axis=1, keepdims=True)
            line = jnp.sum(jnp.where(diag, m, 0.0), axis=0, keepdims=True)
            m_o[g, pl.ds(k, 1), :] = line
            m_o[g, pl.ds(k + X, 1), :] = line

        @pl.when(g < GROUPS - 1)
        def _():
            forward_x(q, g + 1, 1, 0)

        def one(k, c):
            score(lax.rem(k, X))
            return c

        lax.fori_loop(3, 6, one, 0)
        wait(q.at[g, pl.ds(2 * COL, COL)], r_ax.at[0, g, 2])
        score(2)
        for k in range(1, X):
            send(m_o.at[g], m_i.at[g, k - 1], s_st.at[2, g], r_st.at[2, g], at_x(k))
        return c

    forward_x(q, 0, 1, 0)
    lax.fori_loop(0, GROUPS, stage_c, 0)

    def stage_m(g, c):
        wait(m_i.at[g], r_st.at[2, g])
        top = m_o[g]
        for k in range(1, X):
            top = jnp.maximum(top, pltpu.roll(m_i[g, k - 1], k, 0))
        t_o[g] = top
        for k in range(1, Y):
            send(t_o.at[g], t_i.at[g, k - 1], s_st.at[3, g], r_st.at[3, g], at_y(k))
        return c

    lax.fori_loop(0, GROUPS, stage_m, 0)

    def stage_w(g, c):
        wait(t_i.at[g], r_st.at[3, g])
        top = t_o[g]
        for k in range(1, Y):
            top = jnp.maximum(top, pltpu.roll(t_i[g, k - 1], BLK * k, 1))
        m_t[g] = top

        def context(k):
            rows = pl.ds(k * COL, COL)
            m = jnp.sum(jnp.where(diag, m_t[g, pl.ds(k, 1), :], 0.0), axis=1, keepdims=True)
            wb = jnp.exp(s_s[g, rows, :] - m).astype(BF16)
            w[g, rows, :] = wb
            return dot(wb, frames_ref[...], NN)

        rsx_o[g, 2] = context(2)
        scatter_far(rsx_o, rsh_i, g, 9, 0)

        def one(side, c):
            value = context(1 + 2 * side)
            rsx_o[g, side] = value
            rsh[g, side] = rsx_o[g, side, pl.ds(HALF * side, HALF), :]
            scatter_first(rsx_o, rsx_i, g, 9, side)
            return c

        lax.fori_loop(0, 2, one, 0)
        part0[g] = context(0)

        @pl.when(g > 0)
        def _():
            scatter_last(rsx_o, rsx_i, rsh_i, rsh, g - 1, 9, 0)

        return c

    lax.fori_loop(0, GROUPS, stage_w, 0)
    scatter_last(rsx_o, rsx_i, rsh_i, rsh, GROUPS - 1, 9, 0)

    def stage_d(g, c):
        wait(rsx_i.at[g], r_st.at[9, g])
        total = part0[g] + rsx_i[g, 0] + rsx_i[g, 1]
        part0[g, pl.ds(0, BLK), :] = total[:BLK]
        rsy_o[g] = total[BLK:]
        scatter_y(rsy_o, rsy_i, g, 10)
        return c

    lax.fori_loop(0, GROUPS, stage_d, 0)

    def stage_e(g, c):
        wait(rsy_i.at[g], r_st.at[10, g])
        qf = q[g, pl.ds(0, BLK), :].astype(F32).reshape(1, BLK, D)
        rest = rsy_i[g].reshape(Y - 1, BLK, D)
        ctx = part0[g, pl.ds(0, BLK), :].reshape(1, BLK, D) + jnp.sum(rest, axis=0, keepdims=True)
        lane = lax.broadcasted_iota(jnp.int32, (1, BLK, D), 2)
        row = lax.broadcasted_iota(jnp.int32, (1, BLK, D), 1)
        q_norm = lax.rsqrt(jnp.sum(qf * qf, axis=2, keepdims=True) + EPS)
        c_norm = lax.rsqrt(jnp.sum(ctx * ctx, axis=2, keepdims=True) + EPS)
        q_unit = qf * q_norm
        c_unit = ctx * c_norm
        cos = jnp.sum(q_unit * c_unit, axis=2, keepdims=True)
        d_ctx = (q_unit - cos * c_unit) * c_norm
        direct[g] = ((c_unit - cos * q_unit) * q_norm).reshape(BLK, D)
        d_ctx = jnp.where(row == 15, split_row(cos, lane, row), d_ctx).reshape(BLK, D)
        high = d_ctx.astype(BF16)
        uy[g, 0, 0:BLK, :] = high
        uy[g, 0, BLK:, :] = (d_ctx - high.astype(F32)).astype(BF16)
        for k in range(1, Y):
            send(uy.at[g, 0], uy.at[g, k], s_st.at[4, g], r_st.at[4, g], at_y(k))
        return c

    lax.fori_loop(0, GROUPS, stage_e, 0)

    def stage_f(g, c):
        wait(uy.at[g, pl.ds(1, Y - 1)], r_st.at[4, g])
        sums = jnp.sum(uy[g, :, 0:BLK, :].astype(F32)[:, 15, :128], axis=0, keepdims=True)
        col_o[g] = jnp.broadcast_to(sums, (8, 128))
        for k in range(1, X):
            send(col_o.at[g], col_i.at[g, k - 1], s_st.at[8, g], r_st.at[8, g], at_x(k))
        return c

    lax.fori_loop(0, GROUPS, stage_f, 0)

    loss = jnp.zeros((1, 128), F32)
    for g in range(GROUPS):
        wait(col_i.at[g], r_st.at[8, g])
        sums = col_o[g, 0:1, :] + col_i[g, 0, 0:1, :] + col_i[g, 1, 0:1, :] + col_i[g, 2, 0:1, :]
        lane = lax.broadcasted_iota(jnp.int32, (1, 128), 1)
        for s in range(2):
            pick = (lane < 48) & (((lane >> 3) & 1) == s) & ((lane & 7) < 7)
            score = jnp.sum(jnp.where(pick, sums, 0.0), axis=1, keepdims=True) * (1.0 / TOKENS)
            logit = jnp.broadcast_to(TEMP * score + BIAS, (1, 128))
            yes, no = slot_yes[2 * g + s], slot_no[2 * g + s]
            tail = jnp.log1p(jnp.exp(-jnp.abs(logit)))
            loss = loss + yes * (jnp.maximum(-logit, 0.0) + tail) + no * (jnp.maximum(logit, 0.0) + tail)
            pull = yes / (1.0 + jnp.exp(logit)) - no / (1.0 + jnp.exp(-logit))
            gcos[g, pl.ds(8 * s, 8), :] = jnp.broadcast_to(-LOSS_SCALE * TEMP / TOKENS * pull, (8, 128))
        row = lax.broadcasted_iota(jnp.int32, (Y, BLK, 1), 1)
        high = uy[g, :, 0:BLK, :].astype(F32)
        whole = (high + uy[g, :, BLK:, :].astype(F32)) * gcos[g, :, 0:1].reshape(1, BLK, 1)
        u[g, pl.ds(0, COL), :] = jnp.where((row & 7) < 7, whole, 0.0).reshape(COL, D).astype(BF16)
        gather_x(u, g, 5, 1)

    loss_o[...] = jnp.broadcast_to(loss, (8, 128))
    for k in range(1, RECS):
        send(loss_o, loss_i.at[k - 1], s_loss, r_loss, at_r(k))

    forward_x(u, 0, 5, 1)

    def stage_g(g, c):
        @pl.when(g < GROUPS - 1)
        def _():
            forward_x(u, g + 1, 5, 1)

        def back(k):
            rows = pl.ds(k * COL, COL)
            dw = dot(u[g, rows, :], turned[...], NN)
            d = (w[g, rows, :].astype(F32) * dw * SCALE).astype(BF16)
            ds[g, rows, :] = d
            return dot(d, frames_ref[...], NN)

        wait(u.at[g, pl.ds(2 * COL, COL)], r_ax.at[1, g, 2])

        def one(k, c):
            dx_o[g, k - 1] = back(k).astype(BF16)
            scatter_x(dx_o, dx_i, g, k, 6)
            return c

        lax.fori_loop(1, X, one, 0)
        dq0[g] = back(0)
        return c

    lax.fori_loop(0, GROUPS, stage_g, 0)

    def frame_grad(g):
        def tile(n, c):
            cols = pl.ds(pl.multiple_of(n * 512, 512), 512)
            acc = dot(q[g], ds[g, :, cols], TN) + dot(u[g], w[g, :, cols], TN)
            if g:
                acc = acc + gft[:, cols]
            if g < GROUPS - 1:
                gft[:, cols] = acc
            else:
                gf_ref[0, cols, :] = acc.T.astype(BF16)
            return c

        lax.fori_loop(0, FR // 512, tile, 0)

    def stage_h(g):
        wait(dx_i.at[g], r_st.at[6, g])
        total = dq0[g]
        for k in range(X - 1):
            total = total + dx_i[g, k].astype(F32)
        dq0[g] = total
        dy_o[g] = total[BLK:].astype(BF16)
        scatter_y(dy_o, dy_i, g, 7)

    def stage_i(g):
        wait(dy_i.at[g], r_st.at[7, g])
        total = dq0[g, pl.ds(0, BLK), :] + direct[g] * gcos[g, :, 0:1]
        total = total + jnp.sum(dy_i[g].astype(F32).reshape(Y - 1, BLK, D), axis=0)
        slots[g] = total

    def send_back():
        for g in range(OWNERS):
            mine = []
            for t in (2 * g, 2 * g + 1):
                mine.append(sum(picks[t][j] * slots[j // 2, 8 * (j % 2) : 8 * (j % 2) + 8, :] for j in range(2 * GROUPS)))
            back_o[g] = jnp.concatenate(mine, axis=0).astype(BF16)
            send(back_o.at[g], back_i.at[g], s_back.at[g], r_back.at[g], at_r(OFFS[g]))

    for g in range(GROUPS - 1):
        stage_h(g)
    frame_grad(0)
    stage_h(GROUPS - 1)
    for g in range(GROUPS - 1):
        stage_i(g)
    for g in range(1, GROUPS - 1):
        frame_grad(g)
    stage_i(GROUPS - 1)
    send_back()
    frame_grad(GROUPS - 1)

    wait(loss_i, r_loss)
    loss_ref[0, 0] = jnp.sum(loss + jnp.sum(loss_i[:, 0, :], axis=0, keepdims=True)) * (1.0 / 128)

    total = None
    for g in range(OWNERS):
        wait(back_i.at[g], r_back.at[g])
        term = back_i[g].astype(F32)
        total = term if total is None else total + term
    gt_ref[0] = total[0:7].astype(BF16)
    gt_ref[1] = total[8:15].astype(BF16)

    for g in range(OWNERS):
        wait(own, s_text.at[g])
        wait(back_o.at[g], s_back.at[g])
    for g in range(GROUPS):
        for st, ref in ((0, dy_i), (1, dx_o), (2, m_i), (3, t_i), (5, dx_o), (6, dx_o), (7, dy_i), (8, col_i), (9, rsx_o), (10, rsy_i)):
            wait(ref.at[g], s_st.at[st, g])
        wait(uy.at[g, pl.ds(1, Y - 1)], s_st.at[4, g])
    wait(loss_i, s_loss)


def step(GROUPS, frames, texts, pair_rec, pair_text, pair_label):
    vmem = pl.BlockSpec(memory_space=pltpu.VMEM)
    smem = pl.BlockSpec(memory_space=pltpu.SMEM)
    dma = pltpu.SemaphoreType.DMA
    v = pltpu.VMEM
    loss, gf, gt = pl.pallas_call(
        functools.partial(kernel, GROUPS),
        out_shape=(
            jax.ShapeDtypeStruct((1, 1), F32),
            jax.ShapeDtypeStruct((1, FR, D), BF16),
            jax.ShapeDtypeStruct((2, 7, D), BF16),
        ),
        in_specs=[smem, smem, smem, pl.BlockSpec(memory_space=pl.ANY), vmem],
        out_specs=(smem, vmem, vmem),
        scratch_shapes=[
            v((FR, D), BF16),
            v((D, FR), BF16),
            v((BLK, D), BF16),
            v((OWNERS, BLK, D), BF16),
            v((GROUPS, BLK, D), F32),
            v((GROUPS, ROWS, D), BF16),
            v((GROUPS, ROWS, FR), BF16),
            v((GROUPS, ROWS, FR), F32),
            v((GROUPS, 8, 128), F32),
            v((GROUPS, X - 1, 8, 128), F32),
            v((GROUPS, 8, 128), F32),
            v((GROUPS, Y - 1, 8, 128), F32),
            v((GROUPS, 8, 128), F32),
            v((GROUPS, COL, D), F32),
            v((GROUPS, X - 1, COL, D), F32),
            v((GROUPS, 2, COL, D), F32),
            v((GROUPS, 2, HALF, D), F32),
            v((GROUPS, 2, HALF, D), F32),
            v((GROUPS, COL - BLK, D), F32),
            v((GROUPS, COL - BLK, D), F32),
            v((GROUPS, BLK, D), F32),
            v((GROUPS, Y, 2 * BLK, D), BF16),
            v((GROUPS, 8, 128), F32),
            v((GROUPS, X - 1, 8, 128), F32),
            v((GROUPS, ROWS, D), BF16),
            v((GROUPS, ROWS, FR), BF16),
            v((GROUPS, COL, D), F32),
            v((GROUPS, X - 1, COL, D), BF16),
            v((GROUPS, X - 1, COL, D), BF16),
            v((GROUPS, COL - BLK, D), BF16),
            v((GROUPS, COL - BLK, D), BF16),
            v((OWNERS, BLK, D), BF16),
            v((OWNERS, BLK, D), BF16),
            v((D, FR), F32),
            v((BLK, D), F32),
            v((GROUPS, BLK, 128), F32),
            v((8, 128), F32),
            v((RECS - 1, 8, 128), F32),
            dma,
            dma((OWNERS,)), dma((OWNERS,)),
            dma((11, GROUPS)), dma((11, GROUPS)),
            dma((2, GROUPS, 3)), dma((1, GROUPS, 2)),
            dma((OWNERS,)), dma((OWNERS,)),
            dma, dma,
        ],
        compiler_params=pltpu.CompilerParams(
            collective_id=GROUPS, has_side_effects=True, vmem_limit_bytes=48 << 20
        ),
        cost_estimate=pl.CostEstimate(flops=7_300_000_000, bytes_accessed=1_700_000, transcendentals=2_400_000),
    )(pair_rec, pair_text, pair_label, frames, texts)
    return (loss.reshape(()), gf, gt)


def body(frames, texts, pair_rec, pair_text, pair_label):
    same = (pair_rec == jnp.arange(RECS)[None, :])[:, :, None] & (pair_text[:, None] == jnp.arange(2 * RECS)[None, :])[:, None, :]
    named = jnp.sum(jnp.any(same, axis=0).astype(jnp.int32), axis=1)
    return lax.cond(
        jnp.max(named) <= 4,
        functools.partial(step, 2),
        functools.partial(step, 3),
        frames, texts, pair_rec, pair_text, pair_label,
    )


def solution(mesh):
    return jax.shard_map(
        body,
        mesh=mesh,
        in_specs=(P("rec", "frame", None), P("rec", "frame", None), P(), P(), P()),
        out_specs=(P(), P("rec", "frame", None), P("rec", "frame", None)),
        check_vma=False,
    )
```

```python
import functools

import jax
import jax.numpy as jnp
from jax import lax
from jax.experimental import pallas as pl
from jax.experimental.pallas import tpu as pltpu
from jax.sharding import PartitionSpec as P

EPS = 1e-06
TEMP = 10.0
BIAS = -1.0
LOSS_SCALE = 2048.0

X, Y = 4, 8
RECS = 16
OFFS = (1, 15, 8)
OWNERS = 3
D = 256
BLK = 16
HALF = Y * BLK // 2
COL = Y * BLK
ROWS = X * COL
TOKENS = 224
FR = 1536
SCALE = D**-0.5
MESH = pl.DeviceIdType.MESH
F32 = jnp.float32
BF16 = jnp.bfloat16

NN = (((1,), (0,)), ((), ()))
TN = (((0,), (0,)), ((), ()))


def dot(a, b, dims):
    return lax.dot_general(a, b, dims, preferred_element_type=F32)


def kernel(
    GROUPS,
    rec_ref, text_ref, label_ref, frames_hbm, texts_ref,
    loss_ref, gf_ref, gt_ref,
    frames_ref, turned, own, texts_i, slots, q, w, s_s, m_o, m_i, t_o, t_i, m_t, part0, rsx_o, rsx_i, rsh, rsh_i, rsy_o, rsy_i, direct, uy, cos_o, cos_i, col_o, col_i, u, ds, dq0,
    dx_o, dx_i, dy_o, dy_i, back_o, back_i, gft, pad, gcos, loss_o, loss_i,
    s_frames, s_text, r_text, s_st, r_st, r_ax, r_h, s_back, r_back, s_loss, r_loss,
):
    r, f = lax.axis_index("rec"), lax.axis_index("frame")
    x, y = f // Y, f % Y

    def at_y(k):
        return (r, x * Y + lax.rem(y + k, Y))

    def at_x(k):
        return (r, lax.rem(x + k, X) * Y + y)

    def at_r(k):
        return (lax.rem(r + k, RECS), f)

    load = pltpu.make_async_copy(frames_hbm.at[0], frames_ref, s_frames)
    load.start()
    barrier = pltpu.get_barrier_semaphore()
    for k in range(1, RECS):
        pl.semaphore_signal(barrier, inc=1, device_id=at_r(k), device_id_type=MESH)
    for k in range(1, Y):
        pl.semaphore_signal(barrier, inc=1, device_id=at_y(k), device_id_type=MESH)
    for k in range(1, X):
        pl.semaphore_signal(barrier, inc=1, device_id=at_x(k), device_id_type=MESH)

    pad[...] = jnp.zeros_like(pad)
    pad[0:7, :] = texts_ref[0].astype(F32)
    pad[8:15, :] = texts_ref[1].astype(F32)
    own[...] = pad[...].astype(BF16)

    pl.semaphore_wait(barrier, RECS - 1 + Y - 1 + X - 1)

    def send(src, dst, ss, rs, to):
        pltpu.make_async_remote_copy(src, dst, ss, rs, device_id=to, device_id_type=MESH).start()

    def wait(ref, sem):
        pltpu.make_async_copy(ref, ref, sem).wait()

    def gather_y(buf, g, st):
        for k in range(1, Y):
            send(buf.at[g, pl.ds(0, BLK)], buf.at[g, pl.ds(k * BLK, BLK)], s_st.at[st, g], r_st.at[st, g], at_y(k))

    def gather_x(buf, g, st, i):
        send(buf.at[g, pl.ds(0, COL)], buf.at[g, pl.ds(COL, COL)], s_st.at[st, g], r_ax.at[i, g, 0], at_x(1))
        send(buf.at[g, pl.ds(0, COL)], buf.at[g, pl.ds(3 * COL, COL)], s_st.at[st, g], r_ax.at[i, g, 1], at_x(3))
        send(buf.at[g, pl.ds(0, COL)], buf.at[g, pl.ds(2 * COL, COL)], s_st.at[st, g], r_ax.at[i, g, 2], at_x(2))

    def forward_x(buf, g, st, i):
        wait(buf.at[g, pl.ds(COL, COL)], r_ax.at[i, g, 0])
        wait(buf.at[g, pl.ds(3 * COL, COL)], r_ax.at[i, g, 1])

    def scatter_x(out, into, g, k, st):
        send(out.at[g, k - 1], into.at[g, k - 1], s_st.at[st, g], r_st.at[st, g], at_x(X - k))

    def scatter_far(out, halves, g, st, i):
        send(out.at[g, 2, pl.ds(0, HALF)], halves.at[g, 0], s_st.at[st, g], r_h.at[i, g, 0], at_x(3))
        send(out.at[g, 2, pl.ds(HALF, HALF)], halves.at[g, 1], s_st.at[st, g], r_h.at[i, g, 1], at_x(1))

    def scatter_first(out, into, g, st, side):
        rows = pl.ds(HALF - HALF * side, HALF)
        send(out.at[g, side, rows], into.at[g, side, rows], s_st.at[st, g], r_st.at[st, g], at_x(3 - 2 * side))

    def scatter_last(out, into, halves, mine, g, st, i):
        for side in range(2):
            rows = pl.ds(HALF * side, HALF)
            wait(halves.at[g, side], r_h.at[i, g, side])
            out[g, side, rows, :] = (mine[g, side] + halves[g, side].astype(F32)).astype(out.dtype)
            send(out.at[g, side, rows], into.at[g, side, rows], s_st.at[st, g], r_st.at[st, g], at_x(3 - 2 * side))

    def scatter_y(out, into, g, st):
        for k in range(1, Y):
            send(out.at[g, pl.ds(k * BLK - BLK, BLK)], into.at[g, pl.ds(k * BLK - BLK, BLK)], s_st.at[st, g], r_st.at[st, g], at_y(Y - k))

    for g in range(OWNERS):
        send(own, texts_i.at[g], s_text.at[g], r_text.at[g], at_r(RECS - OFFS[g]))

    def count(p, c):
        rec = rec_ref[p, 0]
        text = text_ref[p]
        label = label_ref[p]
        hop = ((text >> 1) - rec) & (RECS - 1)
        mine = (rec == r).astype(jnp.int32)
        out = []
        for g in range(OWNERS):
            for s in range(2):
                hit = mine * (hop == OFFS[g]).astype(jnp.int32) * ((text & 1) == s).astype(jnp.int32)
                out.append(c[len(out)] + hit * label)
                out.append(c[len(out)] + hit * (1 - label))
        return tuple(out)

    counts = lax.fori_loop(0, 32, count, (jnp.int32(0),) * 12)

    picks, taken = [], jnp.int32(0)
    for t in range(2 * OWNERS):
        named = (counts[2 * t] + counts[2 * t + 1] > 0).astype(jnp.int32)
        picks.append([(named * (taken == j).astype(jnp.int32)).astype(F32) for j in range(2 * GROUPS)])
        taken = taken + named
    slot_yes = [sum(picks[t][j] * counts[2 * t].astype(F32) for t in range(2 * OWNERS)) for j in range(2 * GROUPS)]
    slot_no = [sum(picks[t][j] * counts[2 * t + 1].astype(F32) for t in range(2 * OWNERS)) for j in range(2 * GROUPS)]

    texts = []
    for g in range(OWNERS):
        wait(texts_i.at[g], r_text.at[g])
        both = texts_i[g].astype(F32)
        texts += [both[:8], both[8:]]
    for g in range(GROUPS):
        mine = [sum(picks[t][2 * g + s] * texts[t] for t in range(2 * OWNERS)) for s in range(2)]
        q[g, pl.ds(0, BLK), :] = jnp.concatenate(mine, axis=0).astype(BF16)
        gather_y(q, g, 0)

    load.wait()

    def turn(n, c):
        at = pl.ds(pl.multiple_of(n * 256, 256), 256)
        turned[:, at] = frames_ref[at, :].T
        return c

    lax.fori_loop(0, FR // 256, turn, 0)

    def stage_b(g, c):
        wait(q.at[g, pl.ds(BLK, COL - BLK)], r_st.at[0, g])
        gather_x(q, g, 1, 0)
        return c

    lax.fori_loop(0, GROUPS, stage_b, 0)

    square = (COL, COL)
    diag = lax.broadcasted_iota(jnp.int32, square, 0) == lax.broadcasted_iota(jnp.int32, square, 1)

    def stage_c(g, c):
        def score(k):
            rows = pl.ds(k * COL, COL)
            s = dot(q[g, rows, :], turned[...], NN) * SCALE
            s_s[g, rows, :] = s
            m = jnp.max(s, axis=1, keepdims=True)
            line = jnp.sum(jnp.where(diag, m, 0.0), axis=0, keepdims=True)
            m_o[g, pl.ds(k, 1), :] = line
            m_o[g, pl.ds(k + X, 1), :] = line

        @pl.when(g < GROUPS - 1)
        def _():
            forward_x(q, g + 1, 1, 0)

        def one(k, c):
            score(lax.rem(k, X))
            return c

        lax.fori_loop(3, 6, one, 0)
        wait(q.at[g, pl.ds(2 * COL, COL)], r_ax.at[0, g, 2])
        score(2)
        for k in range(1, X):
            send(m_o.at[g], m_i.at[g, k - 1], s_st.at[2, g], r_st.at[2, g], at_x(k))
        return c

    forward_x(q, 0, 1, 0)
    lax.fori_loop(0, GROUPS, stage_c, 0)

    def stage_m(g, c):
        wait(m_i.at[g], r_st.at[2, g])
        top = m_o[g]
        for k in range(1, X):
            top = jnp.maximum(top, pltpu.roll(m_i[g, k - 1], k, 0))
        t_o[g] = top
        for k in range(1, Y):
            send(t_o.at[g], t_i.at[g, k - 1], s_st.at[3, g], r_st.at[3, g], at_y(k))
        return c

    lax.fori_loop(0, GROUPS, stage_m, 0)

    def stage_w(g, c):
        wait(t_i.at[g], r_st.at[3, g])
        top = t_o[g]
        for k in range(1, Y):
            top = jnp.maximum(top, pltpu.roll(t_i[g, k - 1], BLK * k, 1))
        m_t[g] = top

        def context(k):
            rows = pl.ds(k * COL, COL)
            m = jnp.sum(jnp.where(diag, m_t[g, pl.ds(k, 1), :], 0.0), axis=1, keepdims=True)
            wb = jnp.exp(s_s[g, rows, :] - m).astype(BF16)
            w[g, rows, :] = wb
            return dot(wb, frames_ref[...], NN)

        rsx_o[g, 2] = context(2)
        scatter_far(rsx_o, rsh_i, g, 9, 0)

        def one(side, c):
            value = context(1 + 2 * side)
            rsx_o[g, side] = value
            rsh[g, side] = rsx_o[g, side, pl.ds(HALF * side, HALF), :]
            scatter_first(rsx_o, rsx_i, g, 9, side)
            return c

        lax.fori_loop(0, 2, one, 0)
        part0[g] = context(0)

        @pl.when(g > 0)
        def _():
            scatter_last(rsx_o, rsx_i, rsh_i, rsh, g - 1, 9, 0)

        return c

    lax.fori_loop(0, GROUPS, stage_w, 0)
    scatter_last(rsx_o, rsx_i, rsh_i, rsh, GROUPS - 1, 9, 0)

    def stage_d(g, c):
        wait(rsx_i.at[g], r_st.at[9, g])
        total = part0[g] + rsx_i[g, 0] + rsx_i[g, 1]
        part0[g, pl.ds(0, BLK), :] = total[:BLK]
        rsy_o[g] = total[BLK:]
        scatter_y(rsy_o, rsy_i, g, 10)
        return c

    lax.fori_loop(0, GROUPS, stage_d, 0)

    def stage_e(g, c):
        wait(rsy_i.at[g], r_st.at[10, g])
        qf = q[g, pl.ds(0, BLK), :].astype(F32).reshape(1, BLK, D)
        rest = rsy_i[g].reshape(Y - 1, BLK, D)
        ctx = part0[g, pl.ds(0, BLK), :].reshape(1, BLK, D) + jnp.sum(rest, axis=0, keepdims=True)
        lane = lax.broadcasted_iota(jnp.int32, (1, BLK, D), 2)
        row = lax.broadcasted_iota(jnp.int32, (1, BLK, D), 1)
        q_norm = lax.rsqrt(jnp.sum(qf * qf, axis=2, keepdims=True) + EPS)
        c_norm = lax.rsqrt(jnp.sum(ctx * ctx, axis=2, keepdims=True) + EPS)
        q_unit = qf * q_norm
        c_unit = ctx * c_norm
        cos = jnp.sum(q_unit * c_unit, axis=2, keepdims=True)
        line = jnp.sum(jnp.where(lane[:, :, :128] == row[:, :, :128], cos, 0.0), axis=1)
        cos_o[g] = jnp.broadcast_to(line, (8, 128))
        for k in range(1, Y):
            send(cos_o.at[g], cos_i.at[g, k - 1], s_st.at[11, g], r_st.at[11, g], at_y(k))
        d_ctx = ((q_unit - cos * c_unit) * c_norm).reshape(BLK, D)
        direct[g] = ((c_unit - cos * q_unit) * q_norm).reshape(BLK, D)
        high = d_ctx.astype(BF16)
        uy[g, 0, 0:BLK, :] = high
        uy[g, 0, BLK:, :] = (d_ctx - high.astype(F32)).astype(BF16)
        for k in range(1, Y):
            send(uy.at[g, 0], uy.at[g, k], s_st.at[4, g], r_st.at[4, g], at_y(k))
        return c

    lax.fori_loop(0, GROUPS, stage_e, 0)

    def stage_f(g, c):
        wait(cos_i.at[g], r_st.at[11, g])
        sums = cos_o[g, 0:1, :] + jnp.sum(cos_i[g, :, 0, :], axis=0, keepdims=True)
        col_o[g] = jnp.broadcast_to(sums, (8, 128))
        for k in range(1, X):
            send(col_o.at[g], col_i.at[g, k - 1], s_st.at[8, g], r_st.at[8, g], at_x(k))
        return c

    lax.fori_loop(0, GROUPS, stage_f, 0)

    loss = jnp.zeros((1, 128), F32)
    for g in range(GROUPS):
        wait(col_i.at[g], r_st.at[8, g])
        sums = col_o[g, 0:1, :] + col_i[g, 0, 0:1, :] + col_i[g, 1, 0:1, :] + col_i[g, 2, 0:1, :]
        lane = lax.broadcasted_iota(jnp.int32, (1, 128), 1)
        for s in range(2):
            pick = ((lane >> 3) == s) & ((lane & 7) < 7)
            score = jnp.sum(jnp.where(pick, sums, 0.0), axis=1, keepdims=True) * (1.0 / TOKENS)
            logit = jnp.broadcast_to(TEMP * score + BIAS, (1, 128))
            yes, no = slot_yes[2 * g + s], slot_no[2 * g + s]
            tail = jnp.log1p(jnp.exp(-jnp.abs(logit)))
            loss = loss + yes * (jnp.maximum(-logit, 0.0) + tail) + no * (jnp.maximum(logit, 0.0) + tail)
            pull = yes / (1.0 + jnp.exp(logit)) - no / (1.0 + jnp.exp(-logit))
            gcos[g, pl.ds(8 * s, 8), :] = jnp.broadcast_to(-LOSS_SCALE * TEMP / TOKENS * pull, (8, 128))
        wait(uy.at[g, pl.ds(1, Y - 1)], r_st.at[4, g])
        row = lax.broadcasted_iota(jnp.int32, (Y, BLK, 1), 1)
        high = uy[g, :, 0:BLK, :].astype(F32)
        whole = (high + uy[g, :, BLK:, :].astype(F32)) * gcos[g, :, 0:1].reshape(1, BLK, 1)
        u[g, pl.ds(0, COL), :] = jnp.where((row & 7) < 7, whole, 0.0).reshape(COL, D).astype(BF16)
        gather_x(u, g, 5, 1)

    loss_o[...] = jnp.broadcast_to(loss, (8, 128))
    for k in range(1, RECS):
        send(loss_o, loss_i.at[k - 1], s_loss, r_loss, at_r(k))

    forward_x(u, 0, 5, 1)

    def stage_g(g, c):
        @pl.when(g < GROUPS - 1)
        def _():
            forward_x(u, g + 1, 5, 1)

        def back(k):
            rows = pl.ds(k * COL, COL)
            dw = dot(u[g, rows, :], turned[...], NN)
            d = (w[g, rows, :].astype(F32) * dw * SCALE).astype(BF16)
            ds[g, rows, :] = d
            return dot(d, frames_ref[...], NN)

        wait(u.at[g, pl.ds(2 * COL, COL)], r_ax.at[1, g, 2])

        def one(k, c):
            dx_o[g, k - 1] = back(k).astype(BF16)
            scatter_x(dx_o, dx_i, g, k, 6)
            return c

        lax.fori_loop(1, X, one, 0)
        dq0[g] = back(0)
        return c

    lax.fori_loop(0, GROUPS, stage_g, 0)

    def frame_grad(g):
        def tile(n, c):
            cols = pl.ds(pl.multiple_of(n * 512, 512), 512)
            acc = dot(q[g], ds[g, :, cols], TN) + dot(u[g], w[g, :, cols], TN)
            if g:
                acc = acc + gft[:, cols]
            if g < GROUPS - 1:
                gft[:, cols] = acc
            else:
                gf_ref[0, cols, :] = acc.T.astype(BF16)
            return c

        lax.fori_loop(0, FR // 512, tile, 0)

    def stage_h(g):
        wait(dx_i.at[g], r_st.at[6, g])
        total = dq0[g]
        for k in range(X - 1):
            total = total + dx_i[g, k].astype(F32)
        dq0[g] = total
        dy_o[g] = total[BLK:].astype(BF16)
        scatter_y(dy_o, dy_i, g, 7)

    def stage_i(g):
        wait(dy_i.at[g], r_st.at[7, g])
        total = dq0[g, pl.ds(0, BLK), :] + direct[g] * gcos[g, :, 0:1]
        total = total + jnp.sum(dy_i[g].astype(F32).reshape(Y - 1, BLK, D), axis=0)
        slots[g] = total

    def send_back():
        for g in range(OWNERS):
            mine = []
            for t in (2 * g, 2 * g + 1):
                mine.append(sum(picks[t][j] * slots[j // 2, 8 * (j % 2) : 8 * (j % 2) + 8, :] for j in range(2 * GROUPS)))
            back_o[g] = jnp.concatenate(mine, axis=0).astype(BF16)
            send(back_o.at[g], back_i.at[g], s_back.at[g], r_back.at[g], at_r(OFFS[g]))

    for g in range(GROUPS - 1):
        stage_h(g)
    frame_grad(0)
    stage_h(GROUPS - 1)
    for g in range(GROUPS - 1):
        stage_i(g)
    for g in range(1, GROUPS - 1):
        frame_grad(g)
    stage_i(GROUPS - 1)
    send_back()
    frame_grad(GROUPS - 1)

    wait(loss_i, r_loss)
    loss_ref[0, 0] = jnp.sum(loss + jnp.sum(loss_i[:, 0, :], axis=0, keepdims=True)) * (1.0 / 128)

    total = None
    for g in range(OWNERS):
        wait(back_i.at[g], r_back.at[g])
        term = back_i[g].astype(F32)
        total = term if total is None else total + term
    gt_ref[0] = total[0:7].astype(BF16)
    gt_ref[1] = total[8:15].astype(BF16)

    for g in range(OWNERS):
        wait(own, s_text.at[g])
        wait(back_o.at[g], s_back.at[g])
    for g in range(GROUPS):
        for st, ref in ((0, dy_i), (1, dx_o), (2, m_i), (3, t_i), (5, dx_o), (6, dx_o), (7, dy_i), (8, col_i), (9, rsx_o), (10, rsy_i), (11, cos_i)):
            wait(ref.at[g], s_st.at[st, g])
        wait(uy.at[g, pl.ds(1, Y - 1)], s_st.at[4, g])
    wait(loss_i, s_loss)


def step(GROUPS, frames, texts, pair_rec, pair_text, pair_label):
    vmem = pl.BlockSpec(memory_space=pltpu.VMEM)
    smem = pl.BlockSpec(memory_space=pltpu.SMEM)
    dma = pltpu.SemaphoreType.DMA
    v = pltpu.VMEM
    loss, gf, gt = pl.pallas_call(
        functools.partial(kernel, GROUPS),
        out_shape=(
            jax.ShapeDtypeStruct((1, 1), F32),
            jax.ShapeDtypeStruct((1, FR, D), BF16),
            jax.ShapeDtypeStruct((2, 7, D), BF16),
        ),
        in_specs=[smem, smem, smem, pl.BlockSpec(memory_space=pl.ANY), vmem],
        out_specs=(smem, vmem, vmem),
        scratch_shapes=[
            v((FR, D), BF16),
            v((D, FR), BF16),
            v((BLK, D), BF16),
            v((OWNERS, BLK, D), BF16),
            v((GROUPS, BLK, D), F32),
            v((GROUPS, ROWS, D), BF16),
            v((GROUPS, ROWS, FR), BF16),
            v((GROUPS, ROWS, FR), F32),
            v((GROUPS, 8, 128), F32),
            v((GROUPS, X - 1, 8, 128), F32),
            v((GROUPS, 8, 128), F32),
            v((GROUPS, Y - 1, 8, 128), F32),
            v((GROUPS, 8, 128), F32),
            v((GROUPS, COL, D), F32),
            v((GROUPS, X - 1, COL, D), F32),
            v((GROUPS, 2, COL, D), F32),
            v((GROUPS, 2, HALF, D), F32),
            v((GROUPS, 2, HALF, D), F32),
            v((GROUPS, COL - BLK, D), F32),
            v((GROUPS, COL - BLK, D), F32),
            v((GROUPS, BLK, D), F32),
            v((GROUPS, Y, 2 * BLK, D), BF16),
            v((GROUPS, 8, 128), F32),
            v((GROUPS, Y - 1, 8, 128), F32),
            v((GROUPS, 8, 128), F32),
            v((GROUPS, X - 1, 8, 128), F32),
            v((GROUPS, ROWS, D), BF16),
            v((GROUPS, ROWS, FR), BF16),
            v((GROUPS, COL, D), F32),
            v((GROUPS, X - 1, COL, D), BF16),
            v((GROUPS, X - 1, COL, D), BF16),
            v((GROUPS, COL - BLK, D), BF16),
            v((GROUPS, COL - BLK, D), BF16),
            v((OWNERS, BLK, D), BF16),
            v((OWNERS, BLK, D), BF16),
            v((D, FR), F32),
            v((BLK, D), F32),
            v((GROUPS, BLK, 128), F32),
            v((8, 128), F32),
            v((RECS - 1, 8, 128), F32),
            dma,
            dma((OWNERS,)), dma((OWNERS,)),
            dma((12, GROUPS)), dma((12, GROUPS)),
            dma((2, GROUPS, 3)), dma((1, GROUPS, 2)),
            dma((OWNERS,)), dma((OWNERS,)),
            dma, dma,
        ],
        compiler_params=pltpu.CompilerParams(
            collective_id=GROUPS, has_side_effects=True, vmem_limit_bytes=48 << 20
        ),
        cost_estimate=pl.CostEstimate(flops=7_300_000_000, bytes_accessed=1_700_000, transcendentals=2_400_000),
    )(pair_rec, pair_text, pair_label, frames, texts)
    return (loss.reshape(()), gf, gt)


def body(frames, texts, pair_rec, pair_text, pair_label):
    same = (pair_rec == jnp.arange(RECS)[None, :])[:, :, None] & (pair_text[:, None] == jnp.arange(2 * RECS)[None, :])[:, None, :]
    named = jnp.sum(jnp.any(same, axis=0).astype(jnp.int32), axis=1)
    return lax.cond(
        jnp.max(named) <= 4,
        functools.partial(step, 2),
        functools.partial(step, 3),
        frames, texts, pair_rec, pair_text, pair_label,
    )


def solution(mesh):
    return jax.shard_map(
        body,
        mesh=mesh,
        in_specs=(P("rec", "frame", None), P("rec", "frame", None), P(), P(), P()),
        out_specs=(P(), P("rec", "frame", None), P("rec", "frame", None)),
        check_vma=False,
    )
```

```python
import functools

import jax
import jax.numpy as jnp
from jax import lax
from jax.experimental import pallas as pl
from jax.experimental.pallas import tpu as pltpu
from jax.sharding import PartitionSpec as P

EPS = 1e-06
TEMP = 10.0
BIAS = -1.0
LOSS_SCALE = 2048.0

X, Y = 4, 8
RECS = 16
OFFS = (1, 15, 8)
OWNERS = 3
D = 256
BLK = 16
HALF = Y * BLK // 2
COL = Y * BLK
ROWS = X * COL
TOKENS = 224
FR = 1536
SCALE = D**-0.5
MESH = pl.DeviceIdType.MESH
F32 = jnp.float32
BF16 = jnp.bfloat16

NN = (((1,), (0,)), ((), ()))
TN = (((0,), (0,)), ((), ()))


def dot(a, b, dims):
    return lax.dot_general(a, b, dims, preferred_element_type=F32)


def kernel(
    GROUPS,
    rec_ref, text_ref, label_ref, frames_hbm, texts_ref,
    loss_ref, gf_ref, gt_ref,
    frames_ref, turned, own, texts_i, slots, q, w, s_s, m_o, m_i, t_o, t_i, m_t, part0, rsx_o, rsx_i, rsh, rsh_i, rsy_o, rsy_i, direct, uy, cos_o, cos_i, col_o, col_i, u, ds, dq0,
    dx_o, dx_i, dy_o, dy_i, back_o, back_i, gft, pad, gcos, loss_o, loss_i,
    s_frames, s_text, r_text, s_st, r_st, r_ax, r_h, s_back, r_back, s_loss, r_loss,
):
    r, f = lax.axis_index("rec"), lax.axis_index("frame")
    x, y = f // Y, f % Y

    def at_y(k):
        return (r, x * Y + lax.rem(y + k, Y))

    def at_x(k):
        return (r, lax.rem(x + k, X) * Y + y)

    def at_r(k):
        return (lax.rem(r + k, RECS), f)

    load = pltpu.make_async_copy(frames_hbm.at[0], frames_ref, s_frames)
    load.start()
    barrier = pltpu.get_barrier_semaphore()
    for k in range(1, RECS):
        pl.semaphore_signal(barrier, inc=1, device_id=at_r(k), device_id_type=MESH)
    for k in range(1, Y):
        pl.semaphore_signal(barrier, inc=1, device_id=at_y(k), device_id_type=MESH)
    for k in range(1, X):
        pl.semaphore_signal(barrier, inc=1, device_id=at_x(k), device_id_type=MESH)

    pad[...] = jnp.zeros_like(pad)
    pad[0:7, :] = texts_ref[0].astype(F32)
    pad[8:15, :] = texts_ref[1].astype(F32)
    own[...] = pad[...].astype(BF16)

    pl.semaphore_wait(barrier, RECS - 1 + Y - 1 + X - 1)

    def send(src, dst, ss, rs, to):
        pltpu.make_async_remote_copy(src, dst, ss, rs, device_id=to, device_id_type=MESH).start()

    def wait(ref, sem):
        pltpu.make_async_copy(ref, ref, sem).wait()

    def gather_y(buf, g, st):
        for k in range(1, Y):
            send(buf.at[g, pl.ds(0, BLK)], buf.at[g, pl.ds(k * BLK, BLK)], s_st.at[st, g], r_st.at[st, g], at_y(k))

    def gather_x(buf, g, st, i):
        send(buf.at[g, pl.ds(0, COL)], buf.at[g, pl.ds(COL, COL)], s_st.at[st, g], r_ax.at[i, g, 0], at_x(1))
        send(buf.at[g, pl.ds(0, COL)], buf.at[g, pl.ds(3 * COL, COL)], s_st.at[st, g], r_ax.at[i, g, 1], at_x(3))
        send(buf.at[g, pl.ds(0, COL)], buf.at[g, pl.ds(2 * COL, COL)], s_st.at[st, g], r_ax.at[i, g, 2], at_x(2))

    def forward_x(buf, g, st, i):
        wait(buf.at[g, pl.ds(COL, COL)], r_ax.at[i, g, 0])
        wait(buf.at[g, pl.ds(3 * COL, COL)], r_ax.at[i, g, 1])

    def scatter_x(out, into, g, k, st):
        send(out.at[g, k - 1], into.at[g, k - 1], s_st.at[st, g], r_st.at[st, g], at_x(X - k))

    def scatter_far(out, halves, g, st, i):
        send(out.at[g, 2, pl.ds(0, HALF)], halves.at[g, 0], s_st.at[st, g], r_h.at[i, g, 0], at_x(3))
        send(out.at[g, 2, pl.ds(HALF, HALF)], halves.at[g, 1], s_st.at[st, g], r_h.at[i, g, 1], at_x(1))

    def scatter_first(out, into, g, st, side):
        rows = pl.ds(HALF - HALF * side, HALF)
        send(out.at[g, side, rows], into.at[g, side, rows], s_st.at[st, g], r_st.at[st, g], at_x(3 - 2 * side))

    def scatter_last(out, into, halves, mine, g, st, i):
        for side in range(2):
            rows = pl.ds(HALF * side, HALF)
            wait(halves.at[g, side], r_h.at[i, g, side])
            out[g, side, rows, :] = (mine[g, side] + halves[g, side].astype(F32)).astype(out.dtype)
            send(out.at[g, side, rows], into.at[g, side, rows], s_st.at[st, g], r_st.at[st, g], at_x(3 - 2 * side))

    def scatter_y(out, into, g, st):
        for k in range(1, Y):
            send(out.at[g, pl.ds(k * BLK - BLK, BLK)], into.at[g, pl.ds(k * BLK - BLK, BLK)], s_st.at[st, g], r_st.at[st, g], at_y(Y - k))

    for g in range(OWNERS):
        send(own, texts_i.at[g], s_text.at[g], r_text.at[g], at_r(RECS - OFFS[g]))

    def count(p, c):
        rec = rec_ref[p, 0]
        text = text_ref[p]
        label = label_ref[p]
        hop = ((text >> 1) - rec) & (RECS - 1)
        mine = (rec == r).astype(jnp.int32)
        out = []
        for g in range(OWNERS):
            for s in range(2):
                hit = mine * (hop == OFFS[g]).astype(jnp.int32) * ((text & 1) == s).astype(jnp.int32)
                out.append(c[len(out)] + hit * label)
                out.append(c[len(out)] + hit * (1 - label))
        return tuple(out)

    counts = lax.fori_loop(0, 32, count, (jnp.int32(0),) * 12)

    picks, taken = [], jnp.int32(0)
    for t in range(2 * OWNERS):
        named = (counts[2 * t] + counts[2 * t + 1] > 0).astype(jnp.int32)
        picks.append([(named * (taken == j).astype(jnp.int32)).astype(F32) for j in range(2 * GROUPS)])
        taken = taken + named
    slot_yes = [sum(picks[t][j] * counts[2 * t].astype(F32) for t in range(2 * OWNERS)) for j in range(2 * GROUPS)]
    slot_no = [sum(picks[t][j] * counts[2 * t + 1].astype(F32) for t in range(2 * OWNERS)) for j in range(2 * GROUPS)]

    texts = []
    for g in range(OWNERS):
        wait(texts_i.at[g], r_text.at[g])
        both = texts_i[g].astype(F32)
        texts += [both[:8], both[8:]]
    for g in range(GROUPS):
        mine = [sum(picks[t][2 * g + s] * texts[t] for t in range(2 * OWNERS)) for s in range(2)]
        q[g, pl.ds(0, BLK), :] = jnp.concatenate(mine, axis=0).astype(BF16)
        gather_y(q, g, 0)

    load.wait()

    def turn(n, c):
        at = pl.ds(pl.multiple_of(n * 256, 256), 256)
        turned[:, at] = frames_ref[at, :].T
        return c

    lax.fori_loop(0, FR // 256, turn, 0)

    def stage_b(g, c):
        wait(q.at[g, pl.ds(BLK, COL - BLK)], r_st.at[0, g])
        gather_x(q, g, 1, 0)
        return c

    lax.fori_loop(0, GROUPS, stage_b, 0)

    square = (COL, COL)
    diag = lax.broadcasted_iota(jnp.int32, square, 0) == lax.broadcasted_iota(jnp.int32, square, 1)

    def stage_c(g, c):
        def score(k):
            rows = pl.ds(k * COL, COL)
            s = dot(q[g, rows, :], turned[...], NN) * SCALE
            s_s[g, rows, :] = s
            m = jnp.max(s, axis=1, keepdims=True)
            line = jnp.sum(jnp.where(diag, m, 0.0), axis=0, keepdims=True)
            m_o[g, pl.ds(k, 1), :] = line
            m_o[g, pl.ds(k + X, 1), :] = line

        @pl.when(g < GROUPS - 1)
        def _():
            forward_x(q, g + 1, 1, 0)

        def one(k, c):
            score(lax.rem(k, X))
            return c

        lax.fori_loop(3, 6, one, 0)
        wait(q.at[g, pl.ds(2 * COL, COL)], r_ax.at[0, g, 2])
        score(2)
        for k in range(1, X):
            send(m_o.at[g], m_i.at[g, k - 1], s_st.at[2, g], r_st.at[2, g], at_x(k))
        return c

    forward_x(q, 0, 1, 0)
    lax.fori_loop(0, GROUPS, stage_c, 0)

    def stage_m(g, c):
        wait(m_i.at[g], r_st.at[2, g])
        top = m_o[g]
        for k in range(1, X):
            top = jnp.maximum(top, pltpu.roll(m_i[g, k - 1], k, 0))
        t_o[g] = top
        for k in range(1, Y):
            send(t_o.at[g], t_i.at[g, k - 1], s_st.at[3, g], r_st.at[3, g], at_y(k))
        return c

    lax.fori_loop(0, GROUPS, stage_m, 0)

    def stage_w(g, c):
        wait(t_i.at[g], r_st.at[3, g])
        top = t_o[g]
        for k in range(1, Y):
            top = jnp.maximum(top, pltpu.roll(t_i[g, k - 1], BLK * k, 1))
        m_t[g] = top

        def context(k):
            rows = pl.ds(k * COL, COL)
            m = jnp.sum(jnp.where(diag, m_t[g, pl.ds(k, 1), :], 0.0), axis=1, keepdims=True)
            wb = jnp.exp(s_s[g, rows, :] - m).astype(BF16)
            w[g, rows, :] = wb
            return dot(wb, frames_ref[...], NN)

        rsx_o[g, 2] = context(2)
        scatter_far(rsx_o, rsh_i, g, 9, 0)

        def one(side, c):
            value = context(1 + 2 * side)
            rsx_o[g, side] = value
            rsh[g, side] = rsx_o[g, side, pl.ds(HALF * side, HALF), :]
            scatter_first(rsx_o, rsx_i, g, 9, side)
            return c

        lax.fori_loop(0, 2, one, 0)

        @pl.when(g > 0)
        def _():
            scatter_last(rsx_o, rsx_i, rsh_i, rsh, g - 1, 9, 0)

        part0[g] = context(0)
        return c

    lax.fori_loop(0, GROUPS, stage_w, 0)
    scatter_last(rsx_o, rsx_i, rsh_i, rsh, GROUPS - 1, 9, 0)

    def stage_d(g, c):
        wait(rsx_i.at[g], r_st.at[9, g])
        total = part0[g] + rsx_i[g, 0] + rsx_i[g, 1]
        part0[g, pl.ds(0, BLK), :] = total[:BLK]
        rsy_o[g] = total[BLK:]
        scatter_y(rsy_o, rsy_i, g, 10)
        return c

    lax.fori_loop(0, GROUPS, stage_d, 0)

    def stage_e(g, c):
        wait(rsy_i.at[g], r_st.at[10, g])
        qf = q[g, pl.ds(0, BLK), :].astype(F32).reshape(1, BLK, D)
        rest = rsy_i[g].reshape(Y - 1, BLK, D)
        ctx = part0[g, pl.ds(0, BLK), :].reshape(1, BLK, D) + jnp.sum(rest, axis=0, keepdims=True)
        lane = lax.broadcasted_iota(jnp.int32, (1, BLK, D), 2)
        row = lax.broadcasted_iota(jnp.int32, (1, BLK, D), 1)
        q_norm = lax.rsqrt(jnp.sum(qf * qf, axis=2, keepdims=True) + EPS)
        c_norm = lax.rsqrt(jnp.sum(ctx * ctx, axis=2, keepdims=True) + EPS)
        q_unit = qf * q_norm
        c_unit = ctx * c_norm
        cos = jnp.sum(q_unit * c_unit, axis=2, keepdims=True)
        line = jnp.sum(jnp.where(lane[:, :, :128] == row[:, :, :128], cos, 0.0), axis=1)
        cos_o[g] = jnp.broadcast_to(line, (8, 128))
        for k in range(1, Y):
            send(cos_o.at[g], cos_i.at[g, k - 1], s_st.at[11, g], r_st.at[11, g], at_y(k))
        d_ctx = ((q_unit - cos * c_unit) * c_norm).reshape(BLK, D)
        direct[g] = ((c_unit - cos * q_unit) * q_norm).reshape(BLK, D)
        high = d_ctx.astype(BF16)
        uy[g, 0, 0:BLK, :] = high
        uy[g, 0, BLK:, :] = (d_ctx - high.astype(F32)).astype(BF16)
        for k in range(1, Y):
            send(uy.at[g, 0], uy.at[g, k], s_st.at[4, g], r_st.at[4, g], at_y(k))
        return c

    lax.fori_loop(0, GROUPS, stage_e, 0)

    def stage_f(g, c):
        wait(cos_i.at[g], r_st.at[11, g])
        sums = cos_o[g, 0:1, :] + jnp.sum(cos_i[g, :, 0, :], axis=0, keepdims=True)
        col_o[g] = jnp.broadcast_to(sums, (8, 128))
        for k in range(1, X):
            send(col_o.at[g], col_i.at[g, k - 1], s_st.at[8, g], r_st.at[8, g], at_x(k))
        return c

    lax.fori_loop(0, GROUPS, stage_f, 0)

    loss = jnp.zeros((1, 128), F32)
    for g in range(GROUPS):
        wait(col_i.at[g], r_st.at[8, g])
        sums = col_o[g, 0:1, :] + col_i[g, 0, 0:1, :] + col_i[g, 1, 0:1, :] + col_i[g, 2, 0:1, :]
        lane = lax.broadcasted_iota(jnp.int32, (1, 128), 1)
        for s in range(2):
            pick = ((lane >> 3) == s) & ((lane & 7) < 7)
            score = jnp.sum(jnp.where(pick, sums, 0.0), axis=1, keepdims=True) * (1.0 / TOKENS)
            logit = jnp.broadcast_to(TEMP * score + BIAS, (1, 128))
            yes, no = slot_yes[2 * g + s], slot_no[2 * g + s]
            tail = jnp.log1p(jnp.exp(-jnp.abs(logit)))
            loss = loss + yes * (jnp.maximum(-logit, 0.0) + tail) + no * (jnp.maximum(logit, 0.0) + tail)
            pull = yes / (1.0 + jnp.exp(logit)) - no / (1.0 + jnp.exp(-logit))
            gcos[g, pl.ds(8 * s, 8), :] = jnp.broadcast_to(-LOSS_SCALE * TEMP / TOKENS * pull, (8, 128))
        wait(uy.at[g, pl.ds(1, Y - 1)], r_st.at[4, g])
        row = lax.broadcasted_iota(jnp.int32, (Y, BLK, 1), 1)
        high = uy[g, :, 0:BLK, :].astype(F32)
        whole = (high + uy[g, :, BLK:, :].astype(F32)) * gcos[g, :, 0:1].reshape(1, BLK, 1)
        u[g, pl.ds(0, COL), :] = jnp.where((row & 7) < 7, whole, 0.0).reshape(COL, D).astype(BF16)
        gather_x(u, g, 5, 1)

    loss_o[...] = jnp.broadcast_to(loss, (8, 128))
    for k in range(1, RECS):
        send(loss_o, loss_i.at[k - 1], s_loss, r_loss, at_r(k))

    forward_x(u, 0, 5, 1)

    def stage_g(g, c):
        @pl.when(g < GROUPS - 1)
        def _():
            forward_x(u, g + 1, 5, 1)

        def back(k):
            rows = pl.ds(k * COL, COL)
            dw = dot(u[g, rows, :], turned[...], NN)
            d = (w[g, rows, :].astype(F32) * dw * SCALE).astype(BF16)
            ds[g, rows, :] = d
            return dot(d, frames_ref[...], NN)

        wait(u.at[g, pl.ds(2 * COL, COL)], r_ax.at[1, g, 2])

        def one(k, c):
            dx_o[g, k - 1] = back(k).astype(BF16)
            scatter_x(dx_o, dx_i, g, k, 6)
            return c

        lax.fori_loop(1, X, one, 0)
        dq0[g] = back(0)
        return c

    lax.fori_loop(0, GROUPS, stage_g, 0)

    def frame_grad(g):
        def tile(n, c):
            cols = pl.ds(pl.multiple_of(n * 512, 512), 512)
            acc = dot(q[g], ds[g, :, cols], TN) + dot(u[g], w[g, :, cols], TN)
            if g:
                acc = acc + gft[:, cols]
            if g < GROUPS - 1:
                gft[:, cols] = acc
            else:
                gf_ref[0, cols, :] = acc.T.astype(BF16)
            return c

        lax.fori_loop(0, FR // 512, tile, 0)

    def stage_h(g):
        wait(dx_i.at[g], r_st.at[6, g])
        total = dq0[g]
        for k in range(X - 1):
            total = total + dx_i[g, k].astype(F32)
        dq0[g] = total
        dy_o[g] = total[BLK:].astype(BF16)
        scatter_y(dy_o, dy_i, g, 7)

    def stage_i(g):
        wait(dy_i.at[g], r_st.at[7, g])
        total = dq0[g, pl.ds(0, BLK), :] + direct[g] * gcos[g, :, 0:1]
        total = total + jnp.sum(dy_i[g].astype(F32).reshape(Y - 1, BLK, D), axis=0)
        slots[g] = total

    def send_back():
        for g in range(OWNERS):
            mine = []
            for t in (2 * g, 2 * g + 1):
                mine.append(sum(picks[t][j] * slots[j // 2, 8 * (j % 2) : 8 * (j % 2) + 8, :] for j in range(2 * GROUPS)))
            back_o[g] = jnp.concatenate(mine, axis=0).astype(BF16)
            send(back_o.at[g], back_i.at[g], s_back.at[g], r_back.at[g], at_r(OFFS[g]))

    for g in range(GROUPS - 1):
        stage_h(g)
    stage_h(GROUPS - 1)
    frame_grad(0)
    for g in range(GROUPS - 1):
        stage_i(g)
    for g in range(1, GROUPS - 1):
        frame_grad(g)
    stage_i(GROUPS - 1)
    send_back()
    frame_grad(GROUPS - 1)

    wait(loss_i, r_loss)
    loss_ref[0, 0] = jnp.sum(loss + jnp.sum(loss_i[:, 0, :], axis=0, keepdims=True)) * (1.0 / 128)

    total = None
    for g in range(OWNERS):
        wait(back_i.at[g], r_back.at[g])
        term = back_i[g].astype(F32)
        total = term if total is None else total + term
    gt_ref[0] = total[0:7].astype(BF16)
    gt_ref[1] = total[8:15].astype(BF16)

    for g in range(OWNERS):
        wait(own, s_text.at[g])
        wait(back_o.at[g], s_back.at[g])
    for g in range(GROUPS):
        for st, ref in ((0, dy_i), (1, dx_o), (2, m_i), (3, t_i), (5, dx_o), (6, dx_o), (7, dy_i), (8, col_i), (9, rsx_o), (10, rsy_i), (11, cos_i)):
            wait(ref.at[g], s_st.at[st, g])
        wait(uy.at[g, pl.ds(1, Y - 1)], s_st.at[4, g])
    wait(loss_i, s_loss)


def step(GROUPS, frames, texts, pair_rec, pair_text, pair_label):
    vmem = pl.BlockSpec(memory_space=pltpu.VMEM)
    smem = pl.BlockSpec(memory_space=pltpu.SMEM)
    dma = pltpu.SemaphoreType.DMA
    v = pltpu.VMEM
    loss, gf, gt = pl.pallas_call(
        functools.partial(kernel, GROUPS),
        out_shape=(
            jax.ShapeDtypeStruct((1, 1), F32),
            jax.ShapeDtypeStruct((1, FR, D), BF16),
            jax.ShapeDtypeStruct((2, 7, D), BF16),
        ),
        in_specs=[smem, smem, smem, pl.BlockSpec(memory_space=pl.ANY), vmem],
        out_specs=(smem, vmem, vmem),
        scratch_shapes=[
            v((FR, D), BF16),
            v((D, FR), BF16),
            v((BLK, D), BF16),
            v((OWNERS, BLK, D), BF16),
            v((GROUPS, BLK, D), F32),
            v((GROUPS, ROWS, D), BF16),
            v((GROUPS, ROWS, FR), BF16),
            v((GROUPS, ROWS, FR), F32),
            v((GROUPS, 8, 128), F32),
            v((GROUPS, X - 1, 8, 128), F32),
            v((GROUPS, 8, 128), F32),
            v((GROUPS, Y - 1, 8, 128), F32),
            v((GROUPS, 8, 128), F32),
            v((GROUPS, COL, D), F32),
            v((GROUPS, X - 1, COL, D), F32),
            v((GROUPS, 2, COL, D), F32),
            v((GROUPS, 2, HALF, D), F32),
            v((GROUPS, 2, HALF, D), F32),
            v((GROUPS, COL - BLK, D), F32),
            v((GROUPS, COL - BLK, D), F32),
            v((GROUPS, BLK, D), F32),
            v((GROUPS, Y, 2 * BLK, D), BF16),
            v((GROUPS, 8, 128), F32),
            v((GROUPS, Y - 1, 8, 128), F32),
            v((GROUPS, 8, 128), F32),
            v((GROUPS, X - 1, 8, 128), F32),
            v((GROUPS, ROWS, D), BF16),
            v((GROUPS, ROWS, FR), BF16),
            v((GROUPS, COL, D), F32),
            v((GROUPS, X - 1, COL, D), BF16),
            v((GROUPS, X - 1, COL, D), BF16),
            v((GROUPS, COL - BLK, D), BF16),
            v((GROUPS, COL - BLK, D), BF16),
            v((OWNERS, BLK, D), BF16),
            v((OWNERS, BLK, D), BF16),
            v((D, FR), F32),
            v((BLK, D), F32),
            v((GROUPS, BLK, 128), F32),
            v((8, 128), F32),
            v((RECS - 1, 8, 128), F32),
            dma,
            dma((OWNERS,)), dma((OWNERS,)),
            dma((12, GROUPS)), dma((12, GROUPS)),
            dma((2, GROUPS, 3)), dma((1, GROUPS, 2)),
            dma((OWNERS,)), dma((OWNERS,)),
            dma, dma,
        ],
        compiler_params=pltpu.CompilerParams(
            collective_id=GROUPS, has_side_effects=True, vmem_limit_bytes=48 << 20
        ),
        cost_estimate=pl.CostEstimate(flops=7_300_000_000, bytes_accessed=1_700_000, transcendentals=2_400_000),
    )(pair_rec, pair_text, pair_label, frames, texts)
    return (loss.reshape(()), gf, gt)


def body(frames, texts, pair_rec, pair_text, pair_label):
    same = (pair_rec == jnp.arange(RECS)[None, :])[:, :, None] & (pair_text[:, None] == jnp.arange(2 * RECS)[None, :])[:, None, :]
    named = jnp.sum(jnp.any(same, axis=0).astype(jnp.int32), axis=1)
    return lax.cond(
        jnp.max(named) <= 4,
        functools.partial(step, 2),
        functools.partial(step, 3),
        frames, texts, pair_rec, pair_text, pair_label,
    )


def solution(mesh):
    return jax.shard_map(
        body,
        mesh=mesh,
        in_specs=(P("rec", "frame", None), P("rec", "frame", None), P(), P(), P()),
        out_specs=(P(), P("rec", "frame", None), P("rec", "frame", None)),
        check_vma=False,
    )
```
